256 devices in a mesh: rows: 8 (over x, core), cols: 32 (over y, z).
Axes of the slice: x: 4, y: 4, z: 8, core: 2. Of those that a mesh axis runs over, the one named last changes fastest.
Arguments:
- left: bfloat16 [32, 16, 4096], P(None, 'rows', 'cols'), may hold values from -6 to 6
- right: bfloat16 [32, 16, 4096], P(None, 'rows', 'cols'), may hold values from -6 to 6
- offsets: int32 [32], P('cols'), may hold values from 0 to 384, as said below
- weight_one: bfloat16 [27, 32, 32], replicated, may hold values from -0.21875 to 0.21875
- bias_one: float32 [32], replicated, may hold values from -0.5 to 0.5
- weight_two: bfloat16 [27, 32, 32], replicated, may hold values from -0.21875 to 0.21875
- bias_two: float32 [32], replicated, may hold values from -0.5 to 0.5
Outputs:
- aggregated: bfloat16 [32, 48, 16, 4096], P(None, None, 'rows', 'cols')
The draws below stay inside these ranges and needn't reach their ends.
Inputs may be any that keep to these rules, and one draw needn't show every extreme that they name: `offsets`: one tile has offset 384 and another has offset 0; the rest are uneven between.
All inputs are finite; a program needn't handle non-finite values.
Results may differ from the reference program's by a relative error of at most 0.0095.
Values may be sent and summed in bfloat16 or wider, within the bound.
No kernel may reach another device: no remote copies, remote signals or barrier semaphores. Data moves between devices by JAX's collectives and lax.ppermute only.
A program may use at most 64 MiB of HBM per device.

```python
import jax
import jax.numpy as jnp
from jax import lax

C = 32
D = 48
RH = 2
CW = 128
OMAX = 384
TILES = 32
H = 16
W = 4096
N_ROWS = 8


def draw_offsets(key, part):
    key = jax.random.fold_in(key, 7)
    first, second, third = jax.random.split(key, 3)
    values = jax.random.randint(first, (TILES,), 0, OMAX + 1)
    highest = jax.random.randint(second, (), 0, TILES)
    lowest = (highest + 1 + jax.random.randint(third, (), 0, TILES - 1)) % TILES
    places = jnp.arange(TILES)
    values = jnp.where(places == highest, OMAX, values)
    values = jnp.where(places == lowest, 0, values)
    return values.astype(jnp.int32)


def levels(own_key, shape, shards, least, largest):
    def one(position, parts):
        steps = jax.random.uniform(jax.random.fold_in(jax.random.fold_in(own_key, 6), position), (parts,), jnp.float32, least / len(shards), largest / len(shards))
        return jnp.repeat(jnp.exp(steps), shape[position] // parts).reshape((-1,) + (1,) * (len(shape) - position - 1))

    loudness = one(*shards[0])
    for cut in shards[1:]:
        loudness = loudness * one(*cut)
    return loudness


def bell_draw(stream_key, dims, width, limit, cuts=(), kind=jnp.bfloat16):
    drawn = jax.random.normal(stream_key, dims, jnp.float32) * width
    if len(cuts) > 0:
        drawn = levels(stream_key, dims, cuts, -0.22, 0.18) * drawn
    return jnp.clip(drawn, min=-limit, max=limit).astype(kind)


def setup_inputs(seed: int = 0) -> dict:
    key_list = jax.random.split(jax.random.key(seed), 8)
    return {
        "left": bell_draw(key_list[0], (C, H, W), 1.0, 6.0, ((1, 8), (2, 32))),
        "right": bell_draw(key_list[1], (C, H, W), 1.0, 6.0, ((1, 8), (2, 32))),
        "offsets": draw_offsets(jax.random.fold_in(key_list[7], 71), 0),
        "weight_one": bell_draw(key_list[3], (27, C, C), (27 * C) ** -0.5, 0.21875),
        "bias_one": jnp.clip(jax.random.uniform(key_list[4], (C,), jnp.float32, -0.5, 0.5), -0.5, 0.5),
        "weight_two": bell_draw(key_list[5], (27, C, C), (27 * C) ** -0.5, 0.21875),
        "bias_two": jnp.clip(jax.random.uniform(key_list[6], (C,), jnp.float32, -0.5, 0.5), -0.5, 0.5),
    }


def correlation(left, right, offsets):
    columns = jnp.arange(W, dtype=jnp.int32)
    shifted = columns - offsets[columns // CW]

    def one_disparity(disparity):
        source = shifted - disparity
        valid = source >= 0
        taken = jnp.take(right, jnp.maximum(source, 0), axis=2)
        product = left.astype(jnp.float32) * taken.astype(jnp.float32)
        return jnp.where(valid[None, None, :], product, 0.0).astype(jnp.bfloat16)

    stacked = lax.map(one_disparity, jnp.arange(D, dtype=jnp.int32))
    return jnp.transpose(stacked, (1, 0, 2, 3))


def convolve(padded, weight):
    channels = weight.shape[1]
    kernel = jnp.transpose(weight.reshape(3, 3, 3, channels, channels), (3, 4, 0, 1, 2))
    return lax.conv_general_dilated(padded[None], kernel, (1, 1, 1), ((1, 1), (0, 0), (0, 0)), dimension_numbers=("NCDHW", "OIDHW", "NCDHW"), preferred_element_type=jnp.float32)[0]


def reference(left, right, offsets, weight_one, bias_one, weight_two, bias_two):
    volume = correlation(left, right, offsets)
    padded_rows = jnp.pad(volume, ((0, 0), (0, 0), (2, 2), (0, 0)))

    def row_block(group):
        block = lax.dynamic_slice_in_dim(padded_rows, group * RH, RH + 4, 2)
        block = jnp.pad(block, ((0, 0), (0, 0), (0, 0), (1, 1)))
        hidden = jnp.maximum(convolve(block, weight_one) + bias_one[:, None, None, None], 0.0)
        row_place = group * RH - 1 + jnp.arange(RH + 2, dtype=jnp.int32)
        inside = (row_place >= 0) & (row_place < H)
        hidden = jnp.where(inside[None, None, :, None], hidden, 0.0).astype(jnp.bfloat16)
        hidden = jnp.pad(hidden, ((0, 0), (0, 0), (0, 0), (1, 1)))
        center = lax.dynamic_slice_in_dim(volume, group * RH, RH, 2)
        result = convolve(hidden, weight_two) + bias_two[:, None, None, None] + center.astype(jnp.float32)
        return result.astype(jnp.bfloat16)

    blocks = lax.map(row_block, jnp.arange(N_ROWS, dtype=jnp.int32))
    return jnp.transpose(blocks, (1, 2, 0, 3, 4)).reshape(C, D, H, W)
```

```python
import jax
import jax.numpy as jnp
from jax import lax
from jax.experimental import pallas as pl
from jax.experimental.pallas import tpu as pltpu
from jax.sharding import PartitionSpec as P

C = 32
D = 48
RH = 2
CW = 128
VR = RH + 4
HR = RH + 2
VD = VR * C
HD = HR * C
OD = RH * C
KK = 768
F32 = jnp.float32
BF16 = jnp.bfloat16
LIMIT = 50 * 1024 * 1024
VMEM = pl.BlockSpec(memory_space=pltpu.VMEM)
SMEM = pl.BlockSpec(memory_space=pltpu.SMEM)


def iota(shape, dim):
    return lax.broadcasted_iota(jnp.int32, shape, dim)


def prepare(w1_ref, w2_ref, b_ref, t1_ref, t2_ref, c1_ref, c2_ref, sel_ref, idp_ref, tmp):
    zero = jnp.zeros((C, C), F32)
    for e in range(3):
        one = {(a, b): w1_ref[9 * a + 3 * b + e].astype(F32) for a in range(3) for b in range(3)}
        two = {(a, b): w2_ref[9 * a + 3 * b + e].astype(F32) for a in range(3) for b in range(3)}
        for d in range(2):
            for r in range(HR):
                parts = [one.get((dl - d, rl - r), zero) for dl in range(4) for rl in range(VR)]
                row = jnp.concatenate(parts, axis=1)
                t1_ref[e, (d * HR + r) * C : (d * HR + r + 1) * C, :] = row.astype(BF16)
        for d in range(4):
            for h in range(RH):
                parts = [two.get((dl - d, rl - h), zero) for dl in range(6) for rl in range(HR)]
                for q in range(6):
                    tmp[q, pl.ds(d * RH + h, C, stride=8), :] = jnp.concatenate(
                        parts[4 * q : 4 * q + 4], axis=1
                    )
        for q in range(6):
            t2_ref[e, :, q * CW : (q + 1) * CW] = tmp[q].astype(BF16)
    for p in range(8):
        c1_ref[p * C : (p + 1) * C, :] = b_ref[0]
        c2_ref[pl.ds(p, C, stride=8), :] = b_ref[1]
    lane = iota((128, 128), 1)
    src = iota((128, 128), 0)
    d = lane // 2
    used = d < D
    left = (lane % 2 == 1) & used
    right = (lane % 2 == 0) & used
    right_of = (
        ((3, 47 - d), (2, 47 - d)),
        ((3, 48 - d), (3, 111 - d)),
        ((1, 48 - d), (3, 112 - d)),
    )
    left_of = (((3, 50), (0, 127)), ((3, 51), (3, 114)), ((0, 0), (3, 115)))
    for e in range(3):
        for which, table in ((0, right_of), (1, left_of)):
            for t in range(4):
                hit = jnp.zeros((128, 128), jnp.bool_)
                for mask, (tile, place) in zip((left, right), table[e]):
                    if tile == t:
                        hit = hit | (mask & (src == place))
                g = 2 * e + which
                sel_ref[t * 128 : (t + 1) * 128, g * 128 : (g + 1) * 128] = jnp.where(
                    hit, 1.0, 0.0
                ).astype(BF16)
    out = iota((256, 256), 0)
    inn = iota((256, 256), 1)
    idp_ref[...] = jnp.where(inn == (out % 8) * C + out // 8, 1.0, 0.0).astype(BF16)


def prepared(weight_one, weight_two, bias):
    return pl.pallas_call(
        prepare,
        out_shape=(
            jax.ShapeDtypeStruct((3, 256, KK), BF16),
            jax.ShapeDtypeStruct((3, 256, KK), BF16),
            jax.ShapeDtypeStruct((256, CW), F32),
            jax.ShapeDtypeStruct((256, CW), F32),
            jax.ShapeDtypeStruct((512, 768), BF16),
            jax.ShapeDtypeStruct((256, 256), BF16),
        ),
        in_specs=[VMEM] * 3,
        out_specs=[VMEM] * 6,
        scratch_shapes=[pltpu.VMEM((6, 256, CW), F32)],
        compiler_params=pltpu.CompilerParams(vmem_limit_bytes=LIMIT),
        name="prepare",
    )(weight_one, weight_two, bias)


def cut(ids_ref, off_ref, r4, r3, r2, xl, xo, xr, out_ref, tiles):
    col = ids_ref[1]
    last = ids_ref[3] - 1
    o = off_ref[0]

    def scalar_of(ref):
        v = ref[128:144, :].astype(F32)
        return jnp.max(v[0:1] * 8.0 + v[1:2]).astype(jnp.int32)

    o_l = scalar_of(xl)
    o_r = scalar_of(xr)
    dst = iota((64, 64), 0)
    src = iota((64, 64), 1)
    perm = jnp.where(src == (dst % C) * RH + dst // C, 1.0, 0.0).astype(BF16)

    def rows(x):
        return jnp.dot(perm, x, preferred_element_type=F32)

    for t, x in enumerate((r4[...], r3[...], r2[...], xl[64:128, :], xo[64:128, :])):
        keep = (col + (t - 4) >= 0).astype(F32)
        tiles[t] = rows(x) * keep
    tiles[5] = rows(xr[64:128, :])
    lane = iota((64, CW), 1)

    def window(start):
        t = start // CW
        s = start % CW
        back = (CW - s) % CW
        a = tiles[t]
        b = tiles[t + 1]
        return t, s, back, pltpu.roll(jnp.where(lane < s, b, a), back, 1)

    t, s, back, one = window(464 - o)
    two = pltpu.roll(jnp.where(lane < s, tiles[t + 2], tiles[t + 1]), back, 1)
    wl = window(463 - o_l)[3]
    wr = window(529 - o_r)[3]
    near = rows(xl[0:64, :]) * (col > 0).astype(F32)
    far = rows(xr[0:64, :]) * (col < last).astype(F32)
    border = jnp.where(lane < 50, wl, jnp.where(lane < 52, pltpu.roll(near, 52, 1), wr))
    border = jnp.where((lane < 114), border, pltpu.roll(far, 114, 1))
    border = jnp.where((lane < 116) & ((lane < 52) | (lane >= 64)), border, 0.0)
    out_ref[0:64, :] = rows(xo[0:64, :]).astype(BF16)
    out_ref[64:128, :] = one.astype(BF16)
    out_ref[128:192, :] = two.astype(BF16)
    out_ref[192:256, :] = border.astype(BF16)


def windows(ids, offsets, r4, r3, r2, xl, xo, xr):
    return pl.pallas_call(
        cut,
        out_shape=jax.ShapeDtypeStruct((256, CW), BF16),
        in_specs=[SMEM, SMEM] + [VMEM] * 6,
        out_specs=VMEM,
        scratch_shapes=[pltpu.VMEM((6, 64, CW), F32)],
        name="windows",
    )(ids, offsets, r4, r3, r2, xl, xo, xr)


def aggregate(
    ids_ref, own, pair, cross, t1, t2, c1, c2, sel, idp, out_ref, vol, vown, hid, zcol, hcol
):
    row = ids_ref[0]
    col = ids_ref[1]
    rows_last = ids_ref[2] - 1
    cols_last = ids_ref[3] - 1
    odd = row % 2 == 1
    no_up = row == 0
    no_down = row == rows_last

    def tile(t):
        part = slice(t * 64, t * 64 + 64)
        p = pair[part, :]
        x = cross[part, :]
        up = jnp.where(odd, p, x)
        down = jnp.where(odd, x, p)
        up = jnp.where(no_up, jnp.zeros_like(up), up)
        down = jnp.where(no_down, jnp.zeros_like(down), down)
        return jnp.concatenate([up, own[part, :], down], axis=0)

    left, win0, win1, edge = (tile(t) for t in range(4))

    sources = jnp.concatenate([left, win0, win1, edge], axis=1)
    picked = jnp.dot(sources, sel[...], preferred_element_type=F32)
    cells = []
    for e in range(3):
        r = picked[:, (2 * e) * CW : (2 * e + 1) * CW]
        lft = picked[:, (2 * e + 1) * CW : (2 * e + 2) * CW]
        cells.append(r * lft)
    zcol[...] = cells[1]
    acc = jnp.zeros((HD, CW), F32)
    zeros = jnp.zeros((VD, CW), BF16)
    for e in range(3):
        z = cells[e]
        rhs = jnp.concatenate(
            [
                pltpu.roll(z, 2, 1).astype(BF16),
                z.astype(BF16),
                pltpu.roll(z, CW - 2, 1).astype(BF16),
                zeros,
            ],
            axis=0,
        )
        acc += jnp.dot(t1[e, 0:HD, :], rhs, preferred_element_type=F32)
    h = jnp.maximum(acc + c1[0:HD, :], 0.0)
    lane = iota((HD, CW), 1)
    hrow = iota((HD, CW), 0) // C
    gone = (no_up & (hrow == 0)) | (no_down & (hrow == HR - 1))
    gone = gone | ((col == 0) & (lane % 2 == 1)) | ((col == cols_last) & (lane % 2 == 0))
    hcol[...] = jnp.where(gone, 0.0, h)

    vlane = iota((VD, CW), 1)
    first = vlane == 0
    lastl = vlane == CW - 1
    l1 = left.astype(F32)
    l0 = pltpu.roll(l1, 1, 1)
    l2 = pltpu.roll(l1, CW - 1, 1)
    w0 = win0.astype(F32)
    w1 = win1.astype(F32)
    pad = jnp.zeros((VD, CW), BF16)
    for e in range(3):
        vol[e, 0:VD, :] = pad
        vol[e, (D + 1) * VD : (D + 2) * VD, :] = pad
        hid[e, 0:HD, :] = pad[0:HD]
        hid[e, (D + 1) * HD : (D + 2) * HD, :] = pad[0:HD]

    def shifted(k):
        return pltpu.roll(jnp.where(vlane < k, w1, w0), (CW - k) % CW, 1)

    def one_disparity(d, carry):
        s0, s1 = carry
        s2 = s1
        s1 = s0
        s0 = shifted(D - 1 - d)
        border = pltpu.roll(zcol[...], (2 * CW - 1 - 2 * d) % CW, 1)
        base = pl.multiple_of((d + 1) * VD, VD)
        mid = (l1 * s1).astype(BF16)
        vol[0, pl.ds(base, VD), :] = jnp.where(first, border, l0 * s0).astype(BF16)
        vol[1, pl.ds(base, VD), :] = mid
        vol[2, pl.ds(base, VD), :] = jnp.where(lastl, border, l2 * s2).astype(BF16)
        vown[pl.ds(pl.multiple_of(d * OD, OD), OD), :] = mid[2 * C : 4 * C]
        return s0, s1

    lax.fori_loop(0, D, one_disparity, (shifted(D), shifted(D + 1)))

    hl = iota((256, CW), 1)
    hr = (iota((256, CW), 0) // C) % HR
    dead = (no_up & (hr == 0)) | (no_down & (hr == HR - 1))
    hfirst = hl == 0
    hlast = hl == CW - 1

    def conv_one(j, carry):
        d0 = j * 4
        acc = jnp.zeros((256, 256), F32)
        for e in range(3):
            a = vol[e, pl.ds(pl.multiple_of(d0 * VD, VD), KK), :]
            b = vol[e, pl.ds(pl.multiple_of((d0 + 2) * VD, VD), KK), :]
            acc += jnp.dot(t1[e], jnp.concatenate([a, b], axis=1), preferred_element_type=F32)
        for i in range(2):
            h = jnp.maximum(acc[:, i * CW : (i + 1) * CW] + c1[...], 0.0)
            h = jnp.where(dead, 0.0, h)
            d = d0 + 2 * i
            border = jnp.concatenate(
                [
                    pltpu.roll(hcol[...], (2 * CW - 1 - 2 * d) % CW, 1),
                    pltpu.roll(hcol[...], (2 * CW - 3 - 2 * d) % CW, 1),
                ],
                axis=0,
            )
            base = pl.multiple_of((d + 1) * HD, HD)
            hid[0, pl.ds(base, 256), :] = jnp.where(hfirst, border, pltpu.roll(h, 1, 1)).astype(BF16)
            hid[1, pl.ds(base, 256), :] = h.astype(BF16)
            hid[2, pl.ds(base, 256), :] = jnp.where(
                hlast, border, pltpu.roll(h, CW - 1, 1)
            ).astype(BF16)
        return carry

    lax.fori_loop(0, D // 4, conv_one, 0)

    def conv_two(j, carry):
        d0 = j * 8
        va = vown[pl.ds(pl.multiple_of(d0 * OD, OD), 256), :]
        vb = vown[pl.ds(pl.multiple_of((d0 + 4) * OD, OD), 256), :]
        acc = jnp.dot(idp[...], jnp.concatenate([va, vb], axis=1), preferred_element_type=F32)
        for e in range(3):
            a = hid[e, pl.ds(pl.multiple_of(d0 * HD, HD), KK), :]
            b = hid[e, pl.ds(pl.multiple_of((d0 + 4) * HD, HD), KK), :]
            acc += jnp.dot(t2[e], jnp.concatenate([a, b], axis=1), preferred_element_type=F32)
        a = (acc[:, 0:CW] + c2[...]).reshape(C, 8, CW)
        b = (acc[:, CW:] + c2[...]).reshape(C, 8, CW)
        out_ref[:, pl.ds(pl.multiple_of(j * 16, 16), 16), :] = jnp.concatenate(
            [a, b], axis=1
        ).astype(BF16)
        return carry

    lax.fori_loop(0, D // 8, conv_two, 0)


def aggregated(ids, own, pair, cross, t1, t2, c1, c2, sel, idp):
    return pl.pallas_call(
        aggregate,
        out_shape=jax.ShapeDtypeStruct((C, D * RH, CW), BF16),
        in_specs=[SMEM] + [VMEM] * 9,
        out_specs=VMEM,
        scratch_shapes=[
            pltpu.VMEM((3, (D + 2) * VD, CW), BF16),
            pltpu.VMEM((D * OD, CW), BF16),
            pltpu.VMEM((3, (D + 2) * HD, CW), BF16),
            pltpu.VMEM((VD, CW), F32),
            pltpu.VMEM((HD, CW), F32),
        ],
        compiler_params=pltpu.CompilerParams(vmem_limit_bytes=LIMIT),
        name="aggregate",
    )(ids, own, pair, cross, t1, t2, c1, c2, sel, idp)


def ring(x, axis, by):
    n = lax.axis_size(axis)
    return lax.ppermute(x, axis, [(i, (i + by) % n) for i in range(n)])


def swap(x, axis, first):
    n = lax.axis_size(axis)
    pairs = []
    for i in range(first, n + first, 2):
        a, b = i % n, (i + 1) % n
        pairs += [(a, b), (b, a)]
    return lax.ppermute(x, axis, pairs)


def body(left, right, offsets, weight_one, bias_one, weight_two, bias_two):
    ids = jnp.stack(
        [
            lax.axis_index("rows"),
            lax.axis_index("cols"),
            lax.axis_size("rows"),
            lax.axis_size("cols"),
        ]
    ).astype(jnp.int32)
    bias = jnp.broadcast_to(jnp.stack([bias_one, bias_two])[:, :, None], (2, C, CW))
    r = right.reshape(C * RH, CW)
    l = left.reshape(C * RH, CW)
    o = offsets[0]
    place = jnp.arange(16, dtype=jnp.int32)[:, None]
    code = jnp.where(place == 0, o // 8, jnp.where(place == 1, o % 8, 0)).astype(BF16)
    x = jnp.concatenate([l, r, jnp.broadcast_to(code, (16, CW))], axis=0)
    r4 = ring(r, "cols", 4)
    r3 = ring(r, "cols", 3)
    r2 = ring(r, "cols", 2)
    xl = ring(x, "cols", 1)
    xr = ring(x, "cols", -1)
    ready = prepared(weight_one, weight_two, bias)
    own = windows(ids, offsets, r4, r3, r2, xl, x, xr)
    pair = swap(own, "rows", 0)
    cross = swap(own, "rows", 1)
    out = aggregated(ids, own, pair, cross, *ready)
    return out.reshape(C, D, RH, CW)


def solution(mesh):
    return jax.shard_map(
        body,
        mesh=mesh,
        in_specs=(P(None, "rows", "cols"), P(None, "rows", "cols"), P("cols"), P(), P(), P(), P()),
        out_specs=P(None, None, "rows", "cols"),
        check_vma=False,
    )
```

```python
import jax
import jax.numpy as jnp
from jax import lax
from jax.experimental import pallas as pl
from jax.experimental.pallas import tpu as pltpu
from jax.sharding import PartitionSpec as P

C = 32
D = 48
RH = 2
CW = 128
VR = RH + 4
HR = RH + 2
VD = VR * C
HD = HR * C
OD = RH * C
KK = 768
F32 = jnp.float32
BF16 = jnp.bfloat16
MIB = 1024 * 1024
VMEM = pl.BlockSpec(memory_space=pltpu.VMEM)
SMEM = pl.BlockSpec(memory_space=pltpu.SMEM)


def iota(shape, dim):
    return lax.broadcasted_iota(jnp.int32, shape, dim)


def prepare(w1_ref, w2_ref, b1_ref, b2_ref, t1_ref, t2_ref, c1_ref, c2_ref, sel_ref, idp_ref, tmp):
    zero = jnp.zeros((C, C), F32)
    for e in range(3):
        one = {(a, b): w1_ref[9 * a + 3 * b + e].astype(F32) for a in range(3) for b in range(3)}
        two = {(a, b): w2_ref[9 * a + 3 * b + e].astype(F32) for a in range(3) for b in range(3)}
        for d in range(2):
            for r in range(HR):
                parts = [one.get((dl - d, rl - r), zero) for dl in range(4) for rl in range(VR)]
                row = jnp.concatenate(parts, axis=1)
                t1_ref[e, (d * HR + r) * C : (d * HR + r + 1) * C, :] = row.astype(BF16)
        for d in range(4):
            for h in range(RH):
                parts = [two.get((dl - d, rl - h), zero) for dl in range(6) for rl in range(HR)]
                for q in range(6):
                    tmp[q, pl.ds(d * RH + h, C, stride=8), :] = jnp.concatenate(
                        parts[4 * q : 4 * q + 4], axis=1
                    )
        for q in range(6):
            t2_ref[e, :, q * CW : (q + 1) * CW] = tmp[q].astype(BF16)
    eye = iota((C, C), 0) == iota((C, C), 1)

    def column(b):
        b = jnp.sum(jnp.where(eye, jnp.broadcast_to(b, (C, C)), 0.0), axis=1, keepdims=True)
        return jnp.broadcast_to(b, (C, CW))

    one, two = column(b1_ref[...]), column(b2_ref[...])
    for p in range(8):
        c1_ref[p * C : (p + 1) * C, :] = one
        c2_ref[pl.ds(p, C, stride=8), :] = two
    lane = iota((128, 128), 1)
    src = iota((128, 128), 0)
    d = lane // 2
    used = d < D
    left = (lane % 2 == 1) & used
    right = (lane % 2 == 0) & used
    right_of = (
        ((3, 47 - d), (2, 47 - d)),
        ((3, 48 - d), (3, 111 - d)),
        ((1, 48 - d), (3, 112 - d)),
    )
    left_of = (((3, 50), (0, 127)), ((3, 51), (3, 114)), ((0, 0), (3, 115)))
    for e in range(3):
        for which, table in ((0, right_of), (1, left_of)):
            for t in range(4):
                hit = jnp.zeros((128, 128), jnp.bool_)
                for mask, (tile, place) in zip((left, right), table[e]):
                    if tile == t:
                        hit = hit | (mask & (src == place))
                g = 2 * e + which
                sel_ref[t * 128 : (t + 1) * 128, g * 128 : (g + 1) * 128] = jnp.where(
                    hit, 1.0, 0.0
                ).astype(BF16)
    out = iota((256, 256), 0)
    inn = iota((256, 256), 1)
    idp_ref[...] = jnp.where(inn == (out % 8) * C + out // 8, 1.0, 0.0).astype(BF16)


def prepared(weight_one, weight_two, bias_one, bias_two):
    return pl.pallas_call(
        prepare,
        out_shape=(
            jax.ShapeDtypeStruct((3, 256, KK), BF16),
            jax.ShapeDtypeStruct((3, 256, KK), BF16),
            jax.ShapeDtypeStruct((256, CW), F32),
            jax.ShapeDtypeStruct((256, CW), F32),
            jax.ShapeDtypeStruct((512, 768), BF16),
            jax.ShapeDtypeStruct((256, 256), BF16),
        ),
        in_specs=[VMEM] * 4,
        out_specs=[VMEM] * 6,
        scratch_shapes=[pltpu.VMEM((6, 256, CW), F32)],
        cost_estimate=pl.CostEstimate(flops=1000000, bytes_accessed=4000000, transcendentals=0),
        compiler_params=pltpu.CompilerParams(vmem_limit_bytes=12 * MIB),
        name="prepare",
    )(weight_one, weight_two, bias_one.reshape(1, C), bias_two.reshape(1, C))


def cut(off_ref, r4, r3, r2, xl, xo, xr, after_ref, out_ref, tiles):
    col = lax.axis_index("cols")
    last = lax.axis_size("cols") - 1
    o = off_ref[0]

    def scalar_of(ref):
        v = ref[128:144, :].astype(F32)
        return jnp.max(v[0:1] * 8.0 + v[1:2]).astype(jnp.int32)

    o_l = scalar_of(xl)
    o_r = scalar_of(xr)
    dst = iota((64, 64), 0)
    src = iota((64, 64), 1)
    perm = jnp.where(src == (dst % C) * RH + dst // C, 1.0, 0.0).astype(BF16)

    def rows(x):
        return jnp.dot(perm, x, preferred_element_type=F32)

    for t, x in enumerate((r4[...], r3[...], r2[...], xl[64:128, :], xo[64:128, :])):
        keep = (col + (t - 4) >= 0).astype(F32)
        tiles[t] = rows(x) * keep
    tiles[5] = rows(xr[64:128, :])
    lane = iota((64, CW), 1)

    def window(start):
        t = start // CW
        s = start % CW
        back = (CW - s) % CW
        a = tiles[t]
        b = tiles[t + 1]
        return t, s, back, pltpu.roll(jnp.where(lane < s, b, a), back, 1)

    t, s, back, one = window(464 - o)
    two = pltpu.roll(jnp.where(lane < s, tiles[t + 2], tiles[t + 1]), back, 1)
    wl = window(463 - o_l)[3]
    wr = window(529 - o_r)[3]
    near = rows(xl[0:64, :]) * (col > 0).astype(F32)
    far = rows(xr[0:64, :]) * (col < last).astype(F32)
    border = jnp.where(lane < 50, wl, jnp.where(lane < 52, pltpu.roll(near, 52, 1), wr))
    border = jnp.where((lane < 114), border, pltpu.roll(far, 114, 1))
    border = jnp.where((lane < 116) & ((lane < 52) | (lane >= 64)), border, 0.0)
    out_ref[0:64, :] = rows(xo[0:64, :]).astype(BF16)
    out_ref[64:128, :] = one.astype(BF16)
    out_ref[128:192, :] = two.astype(BF16)
    out_ref[192:256, :] = border.astype(BF16)


def windows(offsets, r4, r3, r2, xl, xo, xr, after):
    return pl.pallas_call(
        cut,
        out_shape=jax.ShapeDtypeStruct((256, CW), BF16),
        in_specs=[SMEM] + [VMEM] * 6 + [pl.BlockSpec(memory_space=pl.ANY)],
        out_specs=VMEM,
        scratch_shapes=[pltpu.VMEM((6, 64, CW), F32)],
        compiler_params=pltpu.CompilerParams(vmem_limit_bytes=4 * MIB),
        name="windows",
    )(offsets, r4, r3, r2, xl, xo, xr, after)


def aggregate(
    own, pair, cross, t1, t2, c1, c2, sel, idp, out_ref, vol, vown, hid, zcol, hcol
):
    row = lax.axis_index("rows")
    col = lax.axis_index("cols")
    rows_last = lax.axis_size("rows") - 1
    cols_last = lax.axis_size("cols") - 1
    odd = row % 2 == 1
    no_up = row == 0
    no_down = row == rows_last

    def tile(t):
        part = slice(t * 64, t * 64 + 64)
        p = pair[part, :]
        x = cross[part, :]
        up = jnp.where(odd, p, x)
        down = jnp.where(odd, x, p)
        up = jnp.where(no_up, jnp.zeros_like(up), up)
        down = jnp.where(no_down, jnp.zeros_like(down), down)
        return jnp.concatenate([up, own[part, :], down], axis=0)

    left, win0, win1, edge = (tile(t) for t in range(4))

    sources = jnp.concatenate([left, win0, win1, edge], axis=1)
    picked = jnp.dot(sources, sel[...], preferred_element_type=F32)
    cells = []
    for e in range(3):
        r = picked[:, (2 * e) * CW : (2 * e + 1) * CW]
        lft = picked[:, (2 * e + 1) * CW : (2 * e + 2) * CW]
        cells.append(r * lft)
    zcol[...] = cells[1]
    acc = jnp.zeros((HD, CW), F32)
    zeros = jnp.zeros((VD, CW), BF16)
    for e in range(3):
        z = cells[e]
        rhs = jnp.concatenate(
            [
                pltpu.roll(z, 2, 1).astype(BF16),
                z.astype(BF16),
                pltpu.roll(z, CW - 2, 1).astype(BF16),
                zeros,
            ],
            axis=0,
        )
        acc += jnp.dot(t1[e, 0:HD, :], rhs, preferred_element_type=F32)
    h = jnp.maximum(acc + c1[0:HD, :], 0.0)
    lane = iota((HD, CW), 1)
    hrow = iota((HD, CW), 0) // C
    gone = (no_up & (hrow == 0)) | (no_down & (hrow == HR - 1))
    gone = gone | ((col == 0) & (lane % 2 == 1)) | ((col == cols_last) & (lane % 2 == 0))
    hcol[...] = jnp.where(gone, 0.0, h)

    vlane = iota((VD, CW), 1)
    first = vlane == 0
    lastl = vlane == CW - 1
    l1 = left.astype(F32)
    l0 = pltpu.roll(l1, 1, 1)
    l2 = pltpu.roll(l1, CW - 1, 1)
    w0 = win0.astype(F32)
    w1 = win1.astype(F32)
    pad = jnp.zeros((VD, CW), BF16)
    for e in range(3):
        vol[e, 0:VD, :] = pad
        vol[e, (D + 1) * VD : (D + 2) * VD, :] = pad
        hid[e, 0:HD, :] = pad[0:HD]
        hid[e, (D + 1) * HD : (D + 2) * HD, :] = pad[0:HD]

    def shifted(k):
        return pltpu.roll(jnp.where(vlane < k, w1, w0), (CW - k) % CW, 1)

    def one_disparity(d, carry):
        s0, s1 = carry
        s2 = s1
        s1 = s0
        s0 = shifted(D - 1 - d)
        border = pltpu.roll(zcol[...], (2 * CW - 1 - 2 * d) % CW, 1)
        base = pl.multiple_of((d + 1) * VD, VD)
        mid = (l1 * s1).astype(BF16)
        vol[0, pl.ds(base, VD), :] = jnp.where(first, border, l0 * s0).astype(BF16)
        vol[1, pl.ds(base, VD), :] = mid
        vol[2, pl.ds(base, VD), :] = jnp.where(lastl, border, l2 * s2).astype(BF16)
        vown[pl.ds(pl.multiple_of(d * OD, OD), OD), :] = mid[2 * C : 4 * C]
        return s0, s1

    lax.fori_loop(0, D, one_disparity, (shifted(D), shifted(D + 1)), unroll=True)

    hl = iota((256, CW), 1)
    hr = (iota((256, CW), 0) // C) % HR
    dead = (no_up & (hr == 0)) | (no_down & (hr == HR - 1))
    hfirst = hl == 0
    hlast = hl == CW - 1

    def conv_one(j, carry):
        d0 = j * 4
        acc = jnp.zeros((256, 256), F32)
        for e in range(3):
            a = vol[e, pl.ds(pl.multiple_of(d0 * VD, VD), KK), :]
            b = vol[e, pl.ds(pl.multiple_of((d0 + 2) * VD, VD), KK), :]
            acc += jnp.dot(t1[e], jnp.concatenate([a, b], axis=1), preferred_element_type=F32)
        for i in range(2):
            h = jnp.maximum(acc[:, i * CW : (i + 1) * CW] + c1[...], 0.0)
            h = jnp.where(dead, 0.0, h)
            d = d0 + 2 * i
            border = jnp.concatenate(
                [
                    pltpu.roll(hcol[...], (2 * CW - 1 - 2 * d) % CW, 1),
                    pltpu.roll(hcol[...], (2 * CW - 3 - 2 * d) % CW, 1),
                ],
                axis=0,
            )
            base = pl.multiple_of((d + 1) * HD, HD)
            hid[0, pl.ds(base, 256), :] = jnp.where(hfirst, border, pltpu.roll(h, 1, 1)).astype(BF16)
            hid[1, pl.ds(base, 256), :] = h.astype(BF16)
            hid[2, pl.ds(base, 256), :] = jnp.where(
                hlast, border, pltpu.roll(h, CW - 1, 1)
            ).astype(BF16)
        return carry

    lax.fori_loop(0, D // 4, conv_one, 0, unroll=True)

    def conv_two(j, carry):
        d0 = j * 8
        va = vown[pl.ds(pl.multiple_of(d0 * OD, OD), 256), :]
        vb = vown[pl.ds(pl.multiple_of((d0 + 4) * OD, OD), 256), :]
        acc = jnp.dot(idp[...], jnp.concatenate([va, vb], axis=1), preferred_element_type=F32)
        for e in range(3):
            a = hid[e, pl.ds(pl.multiple_of(d0 * HD, HD), KK), :]
            b = hid[e, pl.ds(pl.multiple_of((d0 + 4) * HD, HD), KK), :]
            acc += jnp.dot(t2[e], jnp.concatenate([a, b], axis=1), preferred_element_type=F32)
        a = (acc[:, 0:CW] + c2[...]).reshape(C, 8, CW)
        b = (acc[:, CW:] + c2[...]).reshape(C, 8, CW)
        out_ref[:, pl.ds(pl.multiple_of(j * 16, 16), 16), :] = jnp.concatenate(
            [a, b], axis=1
        ).astype(BF16)
        return carry

    lax.fori_loop(0, D // 8, conv_two, 0, unroll=True)


def aggregated(own, pair, cross, t1, t2, c1, c2, sel, idp):
    return pl.pallas_call(
        aggregate,
        out_shape=jax.ShapeDtypeStruct((C, D * RH, CW), BF16),
        in_specs=[VMEM] * 9,
        out_specs=VMEM,
        scratch_shapes=[
            pltpu.VMEM((3, (D + 2) * VD, CW), BF16),
            pltpu.VMEM((D * OD, CW), BF16),
            pltpu.VMEM((3, (D + 2) * HD, CW), BF16),
            pltpu.VMEM((VD, CW), F32),
            pltpu.VMEM((HD, CW), F32),
        ],
        compiler_params=pltpu.CompilerParams(vmem_limit_bytes=32 * MIB),
        name="aggregate",
    )(own, pair, cross, t1, t2, c1, c2, sel, idp)


def ring(x, axis, by):
    n = lax.axis_size(axis)
    return lax.ppermute(x, axis, [(i, (i + by) % n) for i in range(n)])


def swap(x, axis, first):
    n = lax.axis_size(axis)
    pairs = []
    for i in range(first, n + first, 2):
        a, b = i % n, (i + 1) % n
        pairs += [(a, b), (b, a)]
    return lax.ppermute(x, axis, pairs)


def body(left, right, offsets, weight_one, bias_one, weight_two, bias_two):
    r = right.reshape(C * RH, CW)
    l = left.reshape(C * RH, CW)
    o = offsets[0]
    place = jnp.arange(16, dtype=jnp.int32)[:, None]
    code = jnp.where(place == 0, o // 8, jnp.where(place == 1, o % 8, 0)).astype(BF16)
    x = jnp.concatenate([l, r, jnp.broadcast_to(code, (16, CW))], axis=0)
    r4 = ring(r, "cols", 4)
    r3 = ring(r, "cols", 3)
    r2 = ring(r, "cols", 2)
    xl = ring(x, "cols", 1)
    xr = ring(x, "cols", -1)
    ready = prepared(weight_one, weight_two, bias_one, bias_two)
    own = windows(offsets, r4, r3, r2, xl, x, xr, ready[2])
    pair = swap(own, "rows", 0)
    cross = swap(own, "rows", 1)
    out = aggregated(own, pair, cross, *ready)
    return out.reshape(C, D, RH, CW)


def solution(mesh):
    return jax.shard_map(
        body,
        mesh=mesh,
        in_specs=(P(None, "rows", "cols"), P(None, "rows", "cols"), P("cols"), P(), P(), P(), P()),
        out_specs=P(None, None, "rows", "cols"),
        check_vma=False,
    )
```

```python
import jax
import jax.numpy as jnp
from jax import lax
from jax.experimental import pallas as pl
from jax.experimental.pallas import tpu as pltpu
from jax.sharding import PartitionSpec as P

C = 32
D = 48
RH = 2
CW = 128
VR = RH + 4
HR = RH + 2
VD = VR * C
HD = HR * C
OD = RH * C
KK = 768
KE = 1792
F32 = jnp.float32
BF16 = jnp.bfloat16
MIB = 1024 * 1024
VMEM = pl.BlockSpec(memory_space=pltpu.VMEM)
SMEM = pl.BlockSpec(memory_space=pltpu.SMEM)


def iota(shape, dim):
    return lax.broadcasted_iota(jnp.int32, shape, dim)


def prepare(
    w1_ref, w2_ref, b1_ref, b2_ref, own_ref, halo_ref, edge_ref, mid_ref, ends_ref, c1_ref, c2_ref, sel_ref
):
    zero = jnp.zeros((C, C), F32)

    def taps(ref):
        return {
            (a, b, e): ref[9 * a + 3 * b + e].astype(F32)
            for a in range(3)
            for b in range(3)
            for e in range(3)
        }

    def fill(ref, row, parts):
        for q in range(0, len(parts), 4):
            ref[row : row + C, q * C : (q + 4) * C] = jnp.concatenate(
                parts[q : q + 4], axis=1
            ).astype(BF16)

    one = taps(w1_ref)
    for r in range(HR):
        for d in range(2):
            row = (r * 2 + d) * C

            def band(rows):
                return [
                    one.get((dl - d, rl - r, e), zero)
                    for e in range(3)
                    for dl in range(4)
                    for rl in rows
                ]

            fill(own_ref, row, band((2, 3)))
            fill(halo_ref, row, band((0, 1) if r < 2 else (4, 5)))
        fill(
            edge_ref,
            r * C,
            [
                one.get((a, rl - r, e), zero)
                for e in range(3)
                for a in range(3)
                for rl in range(VR)
            ]
            + [zero] * 2,
        )
    two = taps(w2_ref)
    for d in range(4):
        for h in range(RH):
            row = (d * RH + h) * C

            def band2(deep):
                return [
                    two.get((dl - d, rl - h, e), zero)
                    for e in range(3)
                    for dl in deep
                    for rl in range(HR)
                ]

            fill(mid_ref, row, band2((2, 3)))
            fill(ends_ref, row, band2((0, 1) if d < 2 else (4, 5)))
    eye = iota((C, C), 0) == iota((C, C), 1)

    def column(b):
        b = jnp.sum(jnp.where(eye, jnp.broadcast_to(b, (C, C)), 0.0), axis=1, keepdims=True)
        return jnp.broadcast_to(b, (C, CW))

    one, two = column(b1_ref[...]), column(b2_ref[...])
    for p in range(8):
        c1_ref[p * C : (p + 1) * C, :] = one
        c2_ref[p * C : (p + 1) * C, :] = two
    lane = iota((128, 128), 1)
    src = iota((128, 128), 0)
    d = lane // 2
    used = d < D
    left = (lane % 2 == 1) & used
    right = (lane % 2 == 0) & used
    right_of = (
        ((3, 47 - d), (2, 47 - d)),
        ((3, 48 - d), (3, 111 - d)),
        ((1, 48 - d), (3, 112 - d)),
    )
    left_of = (((3, 50), (0, 127)), ((3, 51), (3, 114)), ((0, 0), (3, 115)))
    for e in range(3):
        for which, table in ((0, right_of), (1, left_of)):
            for t in range(4):
                hit = jnp.zeros((128, 128), jnp.bool_)
                for mask, (tile, place) in zip((left, right), table[e]):
                    if tile == t:
                        hit = hit | (mask & (src == place))
                g = 2 * e + which
                sel_ref[t * 128 : (t + 1) * 128, g * 128 : (g + 1) * 128] = jnp.where(
                    hit, 1.0, 0.0
                ).astype(BF16)


def prepared(weight_one, weight_two, bias_one, bias_two):
    return pl.pallas_call(
        prepare,
        out_shape=(
            jax.ShapeDtypeStruct((256, KK), BF16),
            jax.ShapeDtypeStruct((256, KK), BF16),
            jax.ShapeDtypeStruct((HD, KE), BF16),
            jax.ShapeDtypeStruct((256, KK), BF16),
            jax.ShapeDtypeStruct((256, KK), BF16),
            jax.ShapeDtypeStruct((256, CW), F32),
            jax.ShapeDtypeStruct((256, CW), F32),
            jax.ShapeDtypeStruct((512, 768), BF16),
        ),
        in_specs=[VMEM] * 4,
        out_specs=[VMEM] * 8,
        cost_estimate=pl.CostEstimate(flops=1000000, bytes_accessed=4000000, transcendentals=0),
        compiler_params=pltpu.CompilerParams(vmem_limit_bytes=12 * MIB),
        name="prepare",
    )(weight_one, weight_two, bias_one.reshape(1, C), bias_two.reshape(1, C))


def cut(off_ref, xr, xl, r2, r3, r4, xo, after_ref, out_ref, tiles):
    col = lax.axis_index("cols")
    last = lax.axis_size("cols") - 1
    o = off_ref[0]

    def scalar_of(ref):
        v = ref[128:144, :].astype(F32)
        return jnp.max(v[0:1] * 8.0 + v[1:2]).astype(jnp.int32)

    o_l = scalar_of(xl)
    o_r = scalar_of(xr)
    dst = iota((64, 64), 0)
    src = iota((64, 64), 1)
    perm = jnp.where(src == (dst % C) * RH + dst // C, 1.0, 0.0).astype(BF16)

    def rows(x):
        return jnp.dot(perm, x, preferred_element_type=F32)

    for t, x in enumerate((r4[...], r3[...], r2[...], xl[64:128, :], xo[64:128, :])):
        keep = (col + (t - 4) >= 0).astype(F32)
        tiles[t] = rows(x) * keep
    tiles[5] = rows(xr[64:128, :])
    lane = iota((64, CW), 1)

    def window(start):
        t = start // CW
        s = start % CW
        back = (CW - s) % CW
        a = tiles[t]
        b = tiles[t + 1]
        return t, s, back, pltpu.roll(jnp.where(lane < s, b, a), back, 1)

    t, s, back, one = window(464 - o)
    two = pltpu.roll(jnp.where(lane < s, tiles[t + 2], tiles[t + 1]), back, 1)
    wl = window(463 - o_l)[3]
    wr = window(529 - o_r)[3]
    near = rows(xl[0:64, :]) * (col > 0).astype(F32)
    far = rows(xr[0:64, :]) * (col < last).astype(F32)
    border = jnp.where(lane < 50, wl, jnp.where(lane < 52, pltpu.roll(near, 52, 1), wr))
    border = jnp.where((lane < 114), border, pltpu.roll(far, 114, 1))
    border = jnp.where((lane < 116) & ((lane < 52) | (lane >= 64)), border, 0.0)
    out_ref[0:64, :] = rows(xo[0:64, :]).astype(BF16)
    out_ref[64:128, :] = one.astype(BF16)
    out_ref[128:192, :] = two.astype(BF16)
    out_ref[192:256, :] = border.astype(BF16)


def windows(offsets, xr, xl, r2, r3, r4, xo, after):
    return pl.pallas_call(
        cut,
        out_shape=jax.ShapeDtypeStruct((256, CW), BF16),
        in_specs=[SMEM] + [VMEM] * 6 + [pl.BlockSpec(memory_space=pl.ANY)],
        out_specs=VMEM,
        scratch_shapes=[pltpu.VMEM((6, 64, CW), F32)],
        compiler_params=pltpu.CompilerParams(vmem_limit_bytes=4 * MIB),
        name="windows",
    )(offsets, xr, xl, r2, r3, r4, xo, after)


def aggregate(
    own, pair, cross, t_own, t_halo, t_edge, t_mid, t_ends, c1, c2, sel, out_ref, vol, hid, stage
):
    row = lax.axis_index("rows")
    col = lax.axis_index("cols")
    rows_last = lax.axis_size("rows") - 1
    cols_last = lax.axis_size("cols") - 1
    odd = row % 2 == 1
    no_up = row == 0
    no_down = row == rows_last

    def tile(t):
        part = slice(t * 64, t * 64 + 64)
        p = pair[part, :]
        x = cross[part, :]
        up = jnp.where(odd, p, x)
        down = jnp.where(odd, x, p)
        up = jnp.where(no_up, jnp.zeros_like(up), up)
        down = jnp.where(no_down, jnp.zeros_like(down), down)
        return jnp.concatenate([up, own[part, :], down], axis=0)

    left, win0, win1, edge = (tile(t) for t in range(4))

    sources = jnp.concatenate([left, win0, win1, edge], axis=1)
    picked = jnp.dot(sources, sel[...], preferred_element_type=F32)
    cells = []
    for e in range(3):
        r = picked[:, (2 * e) * CW : (2 * e + 1) * CW]
        lft = picked[:, (2 * e + 1) * CW : (2 * e + 2) * CW]
        cells.append((r * lft).astype(BF16))
    around = []
    for z in cells:
        around += [pltpu.roll(z, 2, 1), z, pltpu.roll(z, CW - 2, 1)]
    around.append(jnp.zeros((KE - 9 * VD, CW), BF16))
    h = jnp.dot(t_edge[...], jnp.concatenate(around, axis=0), preferred_element_type=F32)
    h = jnp.maximum(h + c1[0:HD, :], 0.0)
    lane = iota((HD, CW), 1)
    hrow = iota((HD, CW), 0) // C
    gone = (no_up & (hrow == 0)) | (no_down & (hrow == HR - 1))
    gone = gone | ((col == 0) & (lane % 2 == 1)) | ((col == cols_last) & (lane % 2 == 0))
    hcol = jnp.where(gone, 0.0, h).astype(BF16)
    zcol = cells[1]

    vlane = iota((OD, CW), 1)
    first = vlane == 0
    last = vlane == CW - 1
    pad = jnp.zeros((HD, CW), BF16)
    for e in range(3):
        for g in range(3):
            vol[g, e, 0:OD, :] = pad[0:OD]
            vol[g, e, (D + 1) * OD : (D + 2) * OD, :] = pad[0:OD]
        hid[e, 0:HD, :] = pad
        hid[e, (D + 1) * HD : (D + 2) * HD, :] = pad
    groups = []
    for g in range(3):
        part = slice(g * OD, (g + 1) * OD)
        l1 = left[part]
        groups.append(
            (pltpu.roll(l1, 1, 1), l1, pltpu.roll(l1, CW - 1, 1), win0[part], win1[part], zcol[part])
        )

    def shifted(g, k):
        w0, w1 = groups[g][3:5]
        if k == 0:
            return w0
        return pltpu.roll(jnp.where(vlane < k, w1, w0), CW - k, 1)

    held = {(g, k): shifted(g, k) for g in range(3) for k in (D, D + 1)}

    def disparity(d):
        k = D - 1 - d
        base = (d + 1) * OD
        for g in range(3):
            l0, l1, l2, _, _, z = groups[g]
            held[g, k] = shifted(g, k)
            border = pltpu.roll(z, (2 * CW - 1 - 2 * d) % CW, 1)
            vol[g, 0, base : base + OD, :] = jnp.where(first, border, l0 * held[g, k])
            vol[g, 1, base : base + OD, :] = l1 * held[g, k + 1]
            vol[g, 2, base : base + OD, :] = jnp.where(last, border, l2 * held.pop((g, k + 2)))

    hl = iota((C, CW), 1)
    hfirst = hl == 0
    hlast = hl == CW - 1

    def conv_one(j):
        d0 = j * 4

        def rhs(g):
            return jnp.concatenate(
                [
                    jnp.concatenate(
                        [
                            vol[g, e, d0 * OD : d0 * OD + 256, :],
                            vol[g, e, (d0 + 2) * OD : (d0 + 2) * OD + 256, :],
                        ],
                        axis=1,
                    )
                    for e in range(3)
                ],
                axis=0,
            )

        mine = jnp.dot(t_own[...], rhs(1), preferred_element_type=F32)
        top = jnp.dot(t_halo[0:128, :], rhs(0), preferred_element_type=F32)
        bottom = jnp.dot(t_halo[128:256, :], rhs(2), preferred_element_type=F32)
        for i in range(2):
            cut = slice(i * CW, (i + 1) * CW)
            for dd in range(2):
                d = d0 + 2 * i + dd
                border = pltpu.roll(hcol, (2 * CW - 1 - 2 * d) % CW, 1)
                for r in range(HR):
                    at = (r * 2 + dd) * C
                    halo = top if r < 2 else bottom
                    ha = at % 128
                    h = mine[at : at + C, cut] + halo[ha : ha + C, cut] + c1[0:C, :]
                    h = jnp.maximum(h, 0.0)
                    if r == 0:
                        h = jnp.where(no_up, 0.0, h)
                    if r == HR - 1:
                        h = jnp.where(no_down, 0.0, h)
                    h = h.astype(BF16)
                    b = border[r * C : (r + 1) * C]
                    base = (d + 1) * HD + r * C
                    hid[0, base : base + C, :] = jnp.where(hfirst, b, pltpu.roll(h, 1, 1))
                    hid[1, base : base + C, :] = h
                    hid[2, base : base + C, :] = jnp.where(hlast, b, pltpu.roll(h, CW - 1, 1))

    def conv_two(j):
        d0 = j * 8

        def rhs(i):
            at = (d0 + 2 * i) * HD
            return jnp.concatenate(
                [
                    jnp.concatenate(
                        [hid[e, at : at + 256, :], hid[e, at + 4 * HD : at + 4 * HD + 256, :]], axis=1
                    )
                    for e in range(3)
                ],
                axis=0,
            )

        mid = jnp.dot(t_mid[...], rhs(1), preferred_element_type=F32)
        low = jnp.dot(t_ends[0:128, :], rhs(0), preferred_element_type=F32)
        high = jnp.dot(t_ends[128:256, :], rhs(2), preferred_element_type=F32)
        for i in range(2):
            cut = slice(i * CW, (i + 1) * CW)
            for p in range(8):
                end = low if p < 4 else high
                at = p * C
                ea = at % 128
                v = vol[1, 1, (d0 + 4 * i + 1) * OD + at : (d0 + 4 * i + 1) * OD + at + C, :]
                a = mid[at : at + C, cut] + end[ea : ea + C, cut] + c2[0:C, :] + v.astype(F32)
                stage[j % 2, pl.ds(8 * i + p, C, stride=16), :] = a
        out_ref[:, j * 16 : j * 16 + 16, :] = stage[j % 2].reshape(C, 16, CW).astype(BF16)

    done = 0
    for j in range(D // 4):
        upto = min(D, 4 * j + 5)
        for d in range(done, upto):
            disparity(d)
        done = upto
        conv_one(j)
    for j in range(D // 8):
        conv_two(j)


def aggregated(own, pair, cross, *ready):
    return pl.pallas_call(
        aggregate,
        out_shape=jax.ShapeDtypeStruct((C, D * RH, CW), BF16),
        in_specs=[VMEM] * 11,
        out_specs=VMEM,
        scratch_shapes=[
            pltpu.VMEM((3, 3, (D + 2) * OD, CW), BF16),
            pltpu.VMEM((3, (D + 2) * HD, CW), BF16),
            pltpu.VMEM((2, 512, CW), F32),
        ],
        compiler_params=pltpu.CompilerParams(vmem_limit_bytes=32 * MIB),
        name="aggregate",
    )(own, pair, cross, *ready)


def ring(x, axis, by):
    n = lax.axis_size(axis)
    return lax.ppermute(x, axis, [(i, (i + by) % n) for i in range(n)])


def swap(x, axis, first):
    n = lax.axis_size(axis)
    pairs = []
    for i in range(first, n + first, 2):
        a, b = i % n, (i + 1) % n
        pairs += [(a, b), (b, a)]
    return lax.ppermute(x, axis, pairs)


def body(left, right, offsets, weight_one, bias_one, weight_two, bias_two):
    r = right.reshape(C * RH, CW)
    l = left.reshape(C * RH, CW)
    o = offsets[0]
    place = jnp.arange(16, dtype=jnp.int32)[:, None]
    code = jnp.where(place == 0, o // 8, jnp.where(place == 1, o % 8, 0)).astype(BF16)
    x = jnp.concatenate([l, r, jnp.broadcast_to(code, (16, CW))], axis=0)
    r4 = ring(r, "cols", 4)
    r3 = ring(r, "cols", 3)
    r2 = ring(r, "cols", 2)
    xl = ring(x, "cols", 1)
    xr = ring(x, "cols", -1)
    ready = prepared(weight_one, weight_two, bias_one, bias_two)
    own = windows(offsets, xr, xl, r2, r3, r4, x, ready[5])
    pair = swap(own, "rows", 0)
    cross = swap(own, "rows", 1)
    out = aggregated(own, pair, cross, *ready)
    return out.reshape(C, D, RH, CW)


def solution(mesh):
    return jax.shard_map(
        body,
        mesh=mesh,
        in_specs=(P(None, "rows", "cols"), P(None, "rows", "cols"), P("cols"), P(), P(), P(), P()),
        out_specs=P(None, None, "rows", "cols"),
        check_vma=False,
    )
```

```python
import jax
import jax.numpy as jnp
from jax import lax
from jax.experimental import pallas as pl
from jax.experimental.pallas import tpu as pltpu
from jax.sharding import PartitionSpec as P

C = 32
D = 48
RH = 2
CW = 128
VR = RH + 4
HR = RH + 2
VD = VR * C
HD = HR * C
OD = RH * C
KK = 768
KE = 1792
F32 = jnp.float32
BF16 = jnp.bfloat16
MIB = 1024 * 1024
VMEM = pl.BlockSpec(memory_space=pltpu.VMEM)
SMEM = pl.BlockSpec(memory_space=pltpu.SMEM)


def iota(shape, dim):
    return lax.broadcasted_iota(jnp.int32, shape, dim)


def prepare(
    w_ref, b_ref, own_ref, halo_ref, edge_ref, mid_ref, ends_ref, c1_ref, c2_ref, sel_ref
):
    zero = jnp.zeros((C, C), F32)

    def taps(base):
        return {
            (a, b, e): w_ref[base + 9 * a + 3 * b + e].astype(F32)
            for a in range(3)
            for b in range(3)
            for e in range(3)
        }

    def fill(ref, row, parts):
        for q in range(0, len(parts), 4):
            ref[row : row + C, q * C : (q + 4) * C] = jnp.concatenate(
                parts[q : q + 4], axis=1
            ).astype(BF16)

    one = taps(0)
    for r in range(HR):
        for d in range(2):
            row = (r * 2 + d) * C

            def band(rows):
                return [
                    one.get((dl - d, rl - r, e), zero)
                    for e in range(3)
                    for dl in range(4)
                    for rl in rows
                ]

            fill(own_ref, row, band((2, 3)))
            fill(halo_ref, row, band((0, 1) if r < 2 else (4, 5)))
        fill(
            edge_ref,
            r * C,
            [
                one.get((a, rl - r, e), zero)
                for e in range(3)
                for a in range(3)
                for rl in range(VR)
            ]
            + [zero] * 2,
        )
    two = taps(27)
    for d in range(4):
        for h in range(RH):
            row = (d * RH + h) * C

            def band2(deep):
                return [
                    two.get((dl - d, rl - h, e), zero)
                    for e in range(3)
                    for dl in deep
                    for rl in range(HR)
                ]

            fill(mid_ref, row, band2((2, 3)))
            fill(ends_ref, row, band2((0, 1) if d < 2 else (4, 5)))
    eye = iota((C, C), 0) == iota((C, C), 1)

    def column(b):
        b = jnp.sum(jnp.where(eye, jnp.broadcast_to(b, (C, C)), 0.0), axis=1, keepdims=True)
        return jnp.broadcast_to(b, (C, CW))

    one, two = column(b_ref[0:1, :]), column(b_ref[1:2, :])
    for p in range(8):
        c1_ref[p * C : (p + 1) * C, :] = one
        c2_ref[p * C : (p + 1) * C, :] = two
    lane = iota((128, 128), 1)
    src = iota((128, 128), 0)
    d = lane // 2
    used = d < D
    left = (lane % 2 == 1) & used
    right = (lane % 2 == 0) & used
    right_of = (
        ((3, 47 - d), (2, 47 - d)),
        ((3, 48 - d), (3, 111 - d)),
        ((1, 48 - d), (3, 112 - d)),
    )
    left_of = (((3, 50), (0, 127)), ((3, 51), (3, 114)), ((0, 0), (3, 115)))
    for e in range(3):
        for which, table in ((0, right_of), (1, left_of)):
            for t in range(4):
                hit = jnp.zeros((128, 128), jnp.bool_)
                for mask, (tile, place) in zip((left, right), table[e]):
                    if tile == t:
                        hit = hit | (mask & (src == place))
                g = 2 * e + which
                sel_ref[t * 128 : (t + 1) * 128, g * 128 : (g + 1) * 128] = jnp.where(
                    hit, 1.0, 0.0
                ).astype(BF16)


def prepared(weight_one, weight_two, bias_one, bias_two):
    return pl.pallas_call(
        prepare,
        out_shape=(
            jax.ShapeDtypeStruct((256, KK), BF16),
            jax.ShapeDtypeStruct((256, KK), BF16),
            jax.ShapeDtypeStruct((HD, KE), BF16),
            jax.ShapeDtypeStruct((256, KK), BF16),
            jax.ShapeDtypeStruct((256, KK), BF16),
            jax.ShapeDtypeStruct((256, CW), F32),
            jax.ShapeDtypeStruct((256, CW), F32),
            jax.ShapeDtypeStruct((512, 768), BF16),
        ),
        in_specs=[VMEM] * 2,
        out_specs=[VMEM] * 8,
        cost_estimate=pl.CostEstimate(flops=1000000, bytes_accessed=4000000, transcendentals=0),
        compiler_params=pltpu.CompilerParams(vmem_limit_bytes=12 * MIB),
        name="prepare",
    )(jnp.concatenate([weight_one, weight_two], axis=0), jnp.stack([bias_one, bias_two]))


def pack(off_ref, lr_ref, out_ref):
    out_ref[0:64, :] = lr_ref[64:128, :]
    k = iota((16, CW), 0)
    at = iota((16, CW), 1)
    of_left = ((k < 2) & (at == k + 126)) | ((k >= 2) & (k < 4) & (at == k - 2))
    of_right = (k >= 4) & (k < 6) & (at == k - 4)

    def columns(chosen, rows):
        return lax.dot_general(
            jnp.where(chosen, 1.0, 0.0).astype(BF16),
            rows,
            (((1,), (1,)), ((), ())),
            preferred_element_type=F32,
        )

    edge = columns(of_left, lr_ref[0:64, :]) + columns(of_right, lr_ref[64:128, :])
    o = off_ref[0]
    code = jnp.where(k == 6, o // 8, jnp.where(k == 7, o % 8, 0)).astype(F32)
    edge = jnp.concatenate([edge, jnp.zeros((16, 64), F32)], axis=1) + code
    out_ref[64:80, :] = edge.astype(BF16)


def packed(offsets, lr):
    return pl.pallas_call(
        pack,
        out_shape=jax.ShapeDtypeStruct((80, CW), BF16),
        in_specs=[SMEM, VMEM],
        out_specs=VMEM,
        compiler_params=pltpu.CompilerParams(vmem_limit_bytes=2 * MIB),
        name="pack",
    )(offsets, lr)


def cut(off_ref, xr, xl, x2, x3, x4, xo, lr_ref, after_ref, out_ref, tiles):
    col = lax.axis_index("cols")
    final = lax.axis_size("cols") - 1
    o = off_ref[0]

    def scalar_of(ref):
        v = ref[64:80, :].astype(F32)
        return jnp.max(v[6:7, 64:128] * 8.0 + v[7:8, 64:128]).astype(jnp.int32)

    o_l = scalar_of(xl)
    o_r = scalar_of(xr)
    dst = iota((64, 64), 0)
    src = iota((64, 64), 1)
    perm = jnp.where(src == (dst % C) * RH + dst // C, 1.0, 0.0).astype(BF16)
    k = iota((16, CW), 0)
    at = iota((16, CW), 1)

    def rows(x):
        return jnp.dot(perm, x, preferred_element_type=F32)

    def placed(ref, chosen):
        edge = lax.dot_general(
            ref[64:80, 0:64],
            jnp.where(chosen, 1.0, 0.0).astype(BF16),
            (((0,), (0,)), ((), ())),
            preferred_element_type=F32,
        )
        return rows(edge.astype(BF16))

    for t, x in enumerate((x4, x3, x2, xl, xo)):
        keep = (col + (t - 4) >= 0).astype(F32)
        tiles[t] = rows(x[0:64, :]) * keep
    tiles[5] = placed(xr, (k >= 4) & (k < 6) & (at == k - 4))
    lane = iota((64, CW), 1)

    def window(start):
        t = start // CW
        s = start % CW
        back = (CW - s) % CW
        a = tiles[t]
        b = tiles[t + 1]
        return t, s, back, pltpu.roll(jnp.where(lane < s, b, a), back, 1)

    t, s, back, one = window(464 - o)
    two = pltpu.roll(jnp.where(lane < s, tiles[t + 2], tiles[t + 1]), back, 1)
    wl = window(463 - o_l)[3]
    wr = window(529 - o_r)[3]
    near = placed(xl, (k < 2) & (at == k + 50)) * (col > 0).astype(F32)
    far = placed(xr, (k >= 2) & (k < 4) & (at == k + 112)) * (col < final).astype(F32)
    border = jnp.where(lane < 50, wl, jnp.where(lane < 64, near, jnp.where(lane < 114, wr, far)))
    out_ref[0:64, :] = rows(lr_ref[0:64, :]).astype(BF16)
    out_ref[64:128, :] = one.astype(BF16)
    out_ref[128:192, :] = two.astype(BF16)
    out_ref[192:256, :] = border.astype(BF16)


def windows(offsets, xr, xl, x2, x3, x4, xo, lr, after):
    return pl.pallas_call(
        cut,
        out_shape=jax.ShapeDtypeStruct((256, CW), BF16),
        in_specs=[SMEM] + [VMEM] * 7 + [pl.BlockSpec(memory_space=pl.ANY)],
        out_specs=VMEM,
        scratch_shapes=[pltpu.VMEM((6, 64, CW), F32)],
        compiler_params=pltpu.CompilerParams(vmem_limit_bytes=4 * MIB),
        name="windows",
    )(offsets, xr, xl, x2, x3, x4, xo, lr, after)


def border_cells(tiles, sel):
    picked = jnp.dot(jnp.concatenate(tiles, axis=1), sel, preferred_element_type=F32)
    cells = []
    for e in range(3):
        r = picked[:, (2 * e) * CW : (2 * e + 1) * CW]
        lft = picked[:, (2 * e + 1) * CW : (2 * e + 2) * CW]
        cells.append((r * lft).astype(BF16))
    return cells


class Rows:
    def __init__(self, tiles, cells, refs):
        left, self.win0, self.win1, _ = tiles
        self.l0, self.l1, self.l2 = pltpu.roll(left, 1, 1), left, pltpu.roll(left, CW - 1, 1)
        self.z = cells[1]
        self.refs = refs
        self.lane = iota((OD, CW), 1)
        pad = jnp.zeros((OD, CW), BF16)
        for ref in refs:
            ref[0:OD, :] = pad
            ref[(D + 1) * OD : (D + 2) * OD, :] = pad
        self.held = {k: self.shifted(k) for k in (D, D + 1)}

    def shifted(self, k):
        if k == 0:
            return self.win0
        return pltpu.roll(jnp.where(self.lane < k, self.win1, self.win0), CW - k, 1)

    def disparity(self, d):
        k = D - 1 - d
        base = (d + 1) * OD
        self.held[k] = self.shifted(k)
        border = pltpu.roll(self.z, (2 * CW - 1 - 2 * d) % CW, 1)
        before, here, after = self.refs
        before[base : base + OD, :] = jnp.where(self.lane == 0, border, self.l0 * self.held[k])
        here[base : base + OD, :] = self.l1 * self.held[k + 1]
        after[base : base + OD, :] = jnp.where(
            self.lane == CW - 1, border, self.l2 * self.held.pop(k + 2)
        )


def window_rows(refs, j):
    d0 = j * 4
    return jnp.concatenate(
        [
            jnp.concatenate(
                [ref[d0 * OD : d0 * OD + 256, :], ref[(d0 + 2) * OD : (d0 + 2) * OD + 256, :]], axis=1
            )
            for ref in refs
        ],
        axis=0,
    )


def blocks(groups, conv):
    done = 0
    for j in range(D // 4):
        upto = min(D, 4 * j + 5)
        for d in range(done, upto):
            for g in groups:
                g.disparity(d)
        done = upto
        conv(j)


def begin(own, t_own, sel, vol_ref, cells_ref, acc_ref):
    tiles = [own[t * 64 : t * 64 + 64, :] for t in range(4)]
    cells = border_cells(tiles, sel[...])
    for e in range(3):
        cells_ref[e] = cells[e]
    refs = [vol_ref.at[e] for e in range(3)]

    def conv(j):
        acc_ref[j] = jnp.dot(t_own[...], window_rows(refs, j), preferred_element_type=F32)

    blocks([Rows(tiles, cells, refs)], conv)


def begun(own, t_own, sel):
    return pl.pallas_call(
        begin,
        out_shape=(
            jax.ShapeDtypeStruct((3, (D + 2) * OD, CW), BF16),
            jax.ShapeDtypeStruct((3, OD, CW), BF16),
            jax.ShapeDtypeStruct((D // 4, 256, 256), F32),
        ),
        in_specs=[VMEM] * 3,
        out_specs=[VMEM] * 3,
        cost_estimate=pl.CostEstimate(
            flops=2 * 12 * 256 * 768 * 256, bytes_accessed=6000000, transcendentals=0
        ),
        compiler_params=pltpu.CompilerParams(vmem_limit_bytes=12 * MIB),
        name="begin",
    )(own, t_own, sel)


def aggregate(
    own_vol, own_cells, acc, pair, cross, t_halo, t_edge, t_mid, t_ends, c1, c2, sel, out_ref, vol, hid, stage
):
    row = lax.axis_index("rows")
    col = lax.axis_index("cols")
    rows_last = lax.axis_size("rows") - 1
    cols_last = lax.axis_size("cols") - 1
    odd = row % 2 == 1
    no_up = row == 0
    no_down = row == rows_last

    def tile(t):
        part = slice(t * 64, t * 64 + 64)
        p = pair[part, :]
        x = cross[part, :]
        up = jnp.where(odd, p, x)
        down = jnp.where(odd, x, p)
        up = jnp.where(no_up, jnp.zeros_like(up), up)
        down = jnp.where(no_down, jnp.zeros_like(down), down)
        return up, down

    ups, downs = zip(*(tile(t) for t in range(4)))
    halo_cells = border_cells(
        [jnp.concatenate([u, w], axis=0) for u, w in zip(ups, downs)], sel[...]
    )
    up_cells = [z[0:OD] for z in halo_cells]
    down_cells = [z[OD:] for z in halo_cells]
    up_refs = [vol.at[0, e] for e in range(3)]
    down_refs = [vol.at[1, e] for e in range(3)]

    around = []
    for e in range(3):
        z = jnp.concatenate([up_cells[e], own_cells[e], down_cells[e]], axis=0)
        around += [pltpu.roll(z, 2, 1), z, pltpu.roll(z, CW - 2, 1)]
    around.append(jnp.zeros((KE - 9 * VD, CW), BF16))
    h = jnp.dot(t_edge[...], jnp.concatenate(around, axis=0), preferred_element_type=F32)
    h = jnp.maximum(h + c1[0:HD, :], 0.0)
    lane = iota((HD, CW), 1)
    hrow = iota((HD, CW), 0) // C
    gone = (no_up & (hrow == 0)) | (no_down & (hrow == HR - 1))
    gone = gone | ((col == 0) & (lane % 2 == 1)) | ((col == cols_last) & (lane % 2 == 0))
    hcol = jnp.where(gone, 0.0, h).astype(BF16)

    pad = jnp.zeros((HD, CW), BF16)
    for e in range(3):
        hid[e, 0:HD, :] = pad
        hid[e, (D + 1) * HD : (D + 2) * HD, :] = pad

    hl = iota((C, CW), 1)
    hfirst = hl == 0
    hlast = hl == CW - 1

    def conv_one(j):
        d0 = j * 4
        top = jnp.dot(t_halo[0:128, :], window_rows(up_refs, j), preferred_element_type=F32)
        bottom = jnp.dot(t_halo[128:256, :], window_rows(down_refs, j), preferred_element_type=F32)
        for i in range(2):
            cut = slice(i * CW, (i + 1) * CW)
            for dd in range(2):
                d = d0 + 2 * i + dd
                border = pltpu.roll(hcol, (2 * CW - 1 - 2 * d) % CW, 1)
                for r in range(HR):
                    at = (r * 2 + dd) * C
                    halo = top if r < 2 else bottom
                    ha = at % 128
                    h = acc[j, at : at + C, cut] + halo[ha : ha + C, cut] + c1[0:C, :]
                    h = jnp.maximum(h, 0.0)
                    if r == 0:
                        h = jnp.where(no_up, 0.0, h)
                    if r == HR - 1:
                        h = jnp.where(no_down, 0.0, h)
                    h = h.astype(BF16)
                    b = border[r * C : (r + 1) * C]
                    base = (d + 1) * HD + r * C
                    hid[0, base : base + C, :] = jnp.where(hfirst, b, pltpu.roll(h, 1, 1))
                    hid[1, base : base + C, :] = h
                    hid[2, base : base + C, :] = jnp.where(hlast, b, pltpu.roll(h, CW - 1, 1))

    def conv_two(j):
        d0 = j * 8

        def rhs(i):
            at = (d0 + 2 * i) * HD
            return jnp.concatenate(
                [
                    jnp.concatenate(
                        [hid[e, at : at + 256, :], hid[e, at + 4 * HD : at + 4 * HD + 256, :]], axis=1
                    )
                    for e in range(3)
                ],
                axis=0,
            )

        mid = jnp.dot(t_mid[...], rhs(1), preferred_element_type=F32)
        low = jnp.dot(t_ends[0:128, :], rhs(0), preferred_element_type=F32)
        high = jnp.dot(t_ends[128:256, :], rhs(2), preferred_element_type=F32)
        for i in range(2):
            cut = slice(i * CW, (i + 1) * CW)
            for p in range(8):
                end = low if p < 4 else high
                at = p * C
                ea = at % 128
                v = own_vol[1, (d0 + 4 * i + 1) * OD + at : (d0 + 4 * i + 1) * OD + at + C, :]
                a = mid[at : at + C, cut] + end[ea : ea + C, cut] + c2[0:C, :] + v.astype(F32)
                stage[j % 2, pl.ds(8 * i + p, C, stride=16), :] = a
        out_ref[:, j * 16 : j * 16 + 16, :] = stage[j % 2].reshape(C, 16, CW).astype(BF16)

    blocks([Rows(ups, up_cells, up_refs), Rows(downs, down_cells, down_refs)], conv_one)
    for j in range(D // 8):
        conv_two(j)


def aggregated(first, pair, cross, t_own, *ready):
    return pl.pallas_call(
        aggregate,
        out_shape=jax.ShapeDtypeStruct((C, D * RH, CW), BF16),
        in_specs=[VMEM] * 12,
        out_specs=VMEM,
        scratch_shapes=[
            pltpu.VMEM((2, 3, (D + 2) * OD, CW), BF16),
            pltpu.VMEM((3, (D + 2) * HD, CW), BF16),
            pltpu.VMEM((2, 512, CW), F32),
        ],
        compiler_params=pltpu.CompilerParams(vmem_limit_bytes=32 * MIB),
        name="aggregate",
    )(*first, pair, cross, *ready)


def ring(x, axis, by):
    n = lax.axis_size(axis)
    return lax.ppermute(x, axis, [(i, (i + by) % n) for i in range(n)])


def swap(x, axis, first):
    n = lax.axis_size(axis)
    pairs = []
    for i in range(first, n + first, 2):
        a, b = i % n, (i + 1) % n
        pairs += [(a, b), (b, a)]
    return lax.ppermute(x, axis, pairs)


def body(left, right, offsets, weight_one, bias_one, weight_two, bias_two):
    lr = jnp.concatenate([left.reshape(C * RH, CW), right.reshape(C * RH, CW)], axis=0)
    x = packed(offsets, lr)
    xr = ring(x, "cols", -1)
    xl = ring(x, "cols", 1)
    x2 = ring(x, "cols", 2)
    x3 = ring(x, "cols", 3)
    x4 = ring(x, "cols", 4)
    ready = prepared(weight_one, weight_two, bias_one, bias_two)
    own = windows(offsets, xr, xl, x2, x3, x4, x, lr, ready[5])
    pair = swap(own, "rows", 0)
    cross = swap(own, "rows", 1)
    out = aggregated(begun(own, ready[0], ready[7]), pair, cross, *ready)
    return out.reshape(C, D, RH, CW)


def solution(mesh):
    return jax.shard_map(
        body,
        mesh=mesh,
        in_specs=(P(None, "rows", "cols"), P(None, "rows", "cols"), P("cols"), P(), P(), P(), P()),
        out_specs=P(None, None, "rows", "cols"),
        check_vma=False,
    )
```

```python
import jax
import jax.numpy as jnp
from jax import lax
from jax.experimental import pallas as pl
from jax.experimental.pallas import tpu as pltpu
from jax.sharding import PartitionSpec as P

C = 32
D = 48
RH = 2
CW = 128
VR = RH + 4
HR = RH + 2
VD = VR * C
HD = HR * C
OD = RH * C
KK = 768
KE = 1792
F32 = jnp.float32
BF16 = jnp.bfloat16
MIB = 1024 * 1024
VMEM = pl.BlockSpec(memory_space=pltpu.VMEM)
SMEM = pl.BlockSpec(memory_space=pltpu.SMEM)


def iota(shape, dim):
    return lax.broadcasted_iota(jnp.int32, shape, dim)


def prepare(
    w_ref, b_ref, own_ref, halo_ref, edge_ref, mid_ref, ends_ref, c1_ref, c2_ref, sel_ref
):
    zero = jnp.zeros((C, C), F32)

    def taps(base):
        return {
            (a, b, e): w_ref[base + 9 * a + 3 * b + e].astype(F32)
            for a in range(3)
            for b in range(3)
            for e in range(3)
        }

    def fill(ref, row, parts):
        for q in range(0, len(parts), 4):
            ref[row : row + C, q * C : (q + 4) * C] = jnp.concatenate(
                parts[q : q + 4], axis=1
            ).astype(BF16)

    one = taps(0)
    for r in range(HR):
        for d in range(2):
            row = (r * 2 + d) * C

            def band(rows):
                return [
                    one.get((dl - d, rl - r, e), zero)
                    for e in range(3)
                    for dl in range(4)
                    for rl in rows
                ]

            fill(own_ref, row, band((2, 3)))
            fill(halo_ref, row, band((0, 1) if r < 2 else (4, 5)))
        fill(
            edge_ref,
            r * C,
            [
                one.get((a, rl - r, e), zero)
                for e in range(3)
                for a in range(3)
                for rl in range(VR)
            ]
            + [zero] * 2,
        )
    two = taps(27)
    for d in range(4):
        for h in range(RH):
            row = (d * RH + h) * C

            def band2(deep):
                return [
                    two.get((dl - d, rl - h, e), zero)
                    for e in range(3)
                    for dl in deep
                    for rl in range(HR)
                ]

            fill(mid_ref, row, band2((2, 3)))
            fill(ends_ref, row, band2((0, 1) if d < 2 else (4, 5)))
    eye = iota((C, C), 0) == iota((C, C), 1)

    def column(b):
        b = jnp.sum(jnp.where(eye, jnp.broadcast_to(b, (C, C)), 0.0), axis=1, keepdims=True)
        return jnp.broadcast_to(b, (C, CW))

    one, two = column(b_ref[0:1, :]), column(b_ref[1:2, :])
    for p in range(8):
        c1_ref[p * C : (p + 1) * C, :] = one
        c2_ref[p * C : (p + 1) * C, :] = two
    lane = iota((128, 128), 1)
    src = iota((128, 128), 0)
    d = lane // 2
    used = d < D
    left = (lane % 2 == 1) & used
    right = (lane % 2 == 0) & used
    right_of = (
        ((3, 47 - d), (2, 47 - d)),
        ((3, 48 - d), (3, 111 - d)),
        ((1, 48 - d), (3, 112 - d)),
    )
    left_of = (((3, 50), (0, 127)), ((3, 51), (3, 114)), ((0, 0), (3, 115)))
    for e in range(3):
        for which, table in ((0, right_of), (1, left_of)):
            for t in range(4):
                hit = jnp.zeros((128, 128), jnp.bool_)
                for mask, (tile, place) in zip((left, right), table[e]):
                    if tile == t:
                        hit = hit | (mask & (src == place))
                g = 2 * e + which
                sel_ref[t * 128 : (t + 1) * 128, g * 128 : (g + 1) * 128] = jnp.where(
                    hit, 1.0, 0.0
                ).astype(BF16)


def prepared(weight_one, weight_two, bias_one, bias_two):
    return pl.pallas_call(
        prepare,
        out_shape=(
            jax.ShapeDtypeStruct((256, KK), BF16),
            jax.ShapeDtypeStruct((256, KK), BF16),
            jax.ShapeDtypeStruct((HD, KE), BF16),
            jax.ShapeDtypeStruct((256, KK), BF16),
            jax.ShapeDtypeStruct((256, KK), BF16),
            jax.ShapeDtypeStruct((256, CW), F32),
            jax.ShapeDtypeStruct((256, CW), F32),
            jax.ShapeDtypeStruct((512, 768), BF16),
        ),
        in_specs=[VMEM] * 2,
        out_specs=[VMEM] * 8,
        cost_estimate=pl.CostEstimate(flops=1000000, bytes_accessed=4000000, transcendentals=0),
        compiler_params=pltpu.CompilerParams(vmem_limit_bytes=12 * MIB),
        name="prepare",
    )(jnp.concatenate([weight_one, weight_two], axis=0), jnp.stack([bias_one, bias_two]))


def pack(off_ref, lr_ref, out_ref):
    out_ref[0:64, :] = lr_ref[64:128, :]
    k = iota((16, CW), 0)
    at = iota((16, CW), 1)
    of_left = ((k < 2) & (at == k + 126)) | ((k >= 2) & (k < 4) & (at == k - 2))
    of_right = (k >= 4) & (k < 6) & (at == k - 4)

    def columns(chosen, rows):
        return lax.dot_general(
            jnp.where(chosen, 1.0, 0.0).astype(BF16),
            rows,
            (((1,), (1,)), ((), ())),
            preferred_element_type=F32,
        )

    edge = columns(of_left, lr_ref[0:64, :]) + columns(of_right, lr_ref[64:128, :])
    o = off_ref[0]
    code = jnp.where(k == 6, o // 8, jnp.where(k == 7, o % 8, 0)).astype(F32)
    edge = jnp.concatenate([edge, jnp.zeros((16, 64), F32)], axis=1) + code
    out_ref[64:80, :] = edge.astype(BF16)


def packed(offsets, lr):
    return pl.pallas_call(
        pack,
        out_shape=jax.ShapeDtypeStruct((80, CW), BF16),
        in_specs=[SMEM, VMEM],
        out_specs=VMEM,
        compiler_params=pltpu.CompilerParams(vmem_limit_bytes=2 * MIB),
        name="pack",
    )(offsets, lr)


def cut(off_ref, xr, xl, x2, x3, x4, xo, lr_ref, after_ref, out_ref, tiles):
    col = lax.axis_index("cols")
    final = lax.axis_size("cols") - 1
    o = off_ref[0]

    def scalar_of(ref):
        v = ref[64:80, :].astype(F32)
        return jnp.max(v[6:7, 64:128] * 8.0 + v[7:8, 64:128]).astype(jnp.int32)

    o_l = scalar_of(xl)
    o_r = scalar_of(xr)
    dst = iota((64, 64), 0)
    src = iota((64, 64), 1)
    perm = jnp.where(src == (dst % C) * RH + dst // C, 1.0, 0.0).astype(BF16)
    k = iota((16, CW), 0)
    at = iota((16, CW), 1)

    def rows(x):
        return jnp.dot(perm, x, preferred_element_type=F32)

    def placed(ref, chosen):
        edge = lax.dot_general(
            ref[64:80, 0:64],
            jnp.where(chosen, 1.0, 0.0).astype(BF16),
            (((0,), (0,)), ((), ())),
            preferred_element_type=F32,
        )
        return rows(edge.astype(BF16))

    for t, x in enumerate((x4, x3, x2, xl, xo)):
        keep = (col + (t - 4) >= 0).astype(F32)
        tiles[t] = rows(x[0:64, :]) * keep
    tiles[5] = placed(xr, (k >= 4) & (k < 6) & (at == k - 4))
    lane = iota((64, CW), 1)

    def window(start):
        t = start // CW
        s = start % CW
        back = (CW - s) % CW
        a = tiles[t]
        b = tiles[t + 1]
        return t, s, back, pltpu.roll(jnp.where(lane < s, b, a), back, 1)

    t, s, back, one = window(464 - o)
    two = pltpu.roll(jnp.where(lane < s, tiles[t + 2], tiles[t + 1]), back, 1)
    wl = window(463 - o_l)[3]
    wr = window(529 - o_r)[3]
    near = placed(xl, (k < 2) & (at == k + 50)) * (col > 0).astype(F32)
    far = placed(xr, (k >= 2) & (k < 4) & (at == k + 112)) * (col < final).astype(F32)
    border = jnp.where(lane < 50, wl, jnp.where(lane < 64, near, jnp.where(lane < 114, wr, far)))
    out_ref[0:64, :] = rows(lr_ref[0:64, :]).astype(BF16)
    out_ref[64:128, :] = one.astype(BF16)
    out_ref[128:192, :] = two.astype(BF16)
    out_ref[192:256, :] = border.astype(BF16)


def windows(offsets, xr, xl, x2, x3, x4, xo, lr, after):
    return pl.pallas_call(
        cut,
        out_shape=jax.ShapeDtypeStruct((256, CW), BF16),
        in_specs=[SMEM] + [VMEM] * 7 + [pl.BlockSpec(memory_space=pl.ANY)],
        out_specs=VMEM,
        scratch_shapes=[pltpu.VMEM((6, 64, CW), F32)],
        compiler_params=pltpu.CompilerParams(vmem_limit_bytes=4 * MIB),
        name="windows",
    )(offsets, xr, xl, x2, x3, x4, xo, lr, after)


def border_cells(tiles, sel):
    picked = jnp.dot(jnp.concatenate(tiles, axis=1), sel, preferred_element_type=F32)
    cells = []
    for e in range(3):
        r = picked[:, (2 * e) * CW : (2 * e + 1) * CW]
        lft = picked[:, (2 * e + 1) * CW : (2 * e + 2) * CW]
        cells.append((r * lft).astype(BF16))
    return cells


class Rows:
    def __init__(self, tiles, cells, refs):
        left, self.win0, self.win1, _ = tiles
        self.l0, self.l1, self.l2 = pltpu.roll(left, 1, 1), left, pltpu.roll(left, CW - 1, 1)
        self.z = cells[1]
        self.refs = refs
        self.lane = iota((OD, CW), 1)
        pad = jnp.zeros((OD, CW), BF16)
        for ref in refs:
            ref[0:OD, :] = pad
            ref[(D + 1) * OD : (D + 2) * OD, :] = pad
        self.held = {k: self.shifted(k) for k in (D, D + 1)}

    def shifted(self, k):
        if k == 0:
            return self.win0
        return pltpu.roll(jnp.where(self.lane < k, self.win1, self.win0), CW - k, 1)

    def disparity(self, d):
        k = D - 1 - d
        base = (d + 1) * OD
        self.held[k] = self.shifted(k)
        border = pltpu.roll(self.z, (2 * CW - 1 - 2 * d) % CW, 1)
        before, here, after = self.refs
        before[base : base + OD, :] = jnp.where(self.lane == 0, border, self.l0 * self.held[k])
        here[base : base + OD, :] = self.l1 * self.held[k + 1]
        after[base : base + OD, :] = jnp.where(
            self.lane == CW - 1, border, self.l2 * self.held.pop(k + 2)
        )


def window_rows(refs, j):
    d0 = j * 4
    return jnp.concatenate(
        [
            jnp.concatenate(
                [ref[d0 * OD : d0 * OD + 256, :], ref[(d0 + 2) * OD : (d0 + 2) * OD + 256, :]], axis=1
            )
            for ref in refs
        ],
        axis=0,
    )


def blocks(groups, conv):
    done = 0
    for j in range(D // 4):
        upto = min(D, 4 * j + 5)
        for d in range(done, upto):
            for g in groups:
                g.disparity(d)
        done = upto
        conv(j)


def begin(own, t_own, c1, sel, vol_ref, cells_ref, acc_ref):
    tiles = [own[t * 64 : t * 64 + 64, :] for t in range(4)]
    cells = border_cells(tiles, sel[...])
    for e in range(3):
        cells_ref[e] = cells[e]
    refs = [vol_ref.at[e] for e in range(3)]

    def conv(j):
        y = jnp.dot(t_own[...], window_rows(refs, j), preferred_element_type=F32)
        acc_ref[j] = y + jnp.concatenate([c1[...], c1[...]], axis=1)

    blocks([Rows(tiles, cells, refs)], conv)


def begun(own, t_own, c1, sel):
    return pl.pallas_call(
        begin,
        out_shape=(
            jax.ShapeDtypeStruct((3, (D + 2) * OD, CW), BF16),
            jax.ShapeDtypeStruct((3, OD, CW), BF16),
            jax.ShapeDtypeStruct((D // 4, 256, 256), F32),
        ),
        in_specs=[VMEM] * 4,
        out_specs=[VMEM] * 3,
        cost_estimate=pl.CostEstimate(
            flops=2 * 12 * 256 * 768 * 256, bytes_accessed=6000000, transcendentals=0
        ),
        compiler_params=pltpu.CompilerParams(vmem_limit_bytes=12 * MIB),
        name="begin",
    )(own, t_own, c1, sel)


def aggregate(
    own_vol,
    own_cells,
    acc,
    pair,
    cross,
    t_halo,
    t_edge,
    t_mid,
    t_ends,
    c1,
    c2,
    sel,
    out_ref,
    vol,
    hid,
    ready,
    sems,
):
    row = lax.axis_index("rows")
    col = lax.axis_index("cols")
    rows_last = lax.axis_size("rows") - 1
    cols_last = lax.axis_size("cols") - 1
    odd = row % 2 == 1
    no_up = row == 0
    no_down = row == rows_last

    def tile(t):
        part = slice(t * 64, t * 64 + 64)
        p = pair[part, :]
        x = cross[part, :]
        up = jnp.where(odd, p, x)
        down = jnp.where(odd, x, p)
        up = jnp.where(no_up, jnp.zeros_like(up), up)
        down = jnp.where(no_down, jnp.zeros_like(down), down)
        return up, down

    ups, downs = zip(*(tile(t) for t in range(4)))
    halo_cells = border_cells(
        [jnp.concatenate([u, w], axis=0) for u, w in zip(ups, downs)], sel[...]
    )
    up_cells = [z[0:OD] for z in halo_cells]
    down_cells = [z[OD:] for z in halo_cells]
    up_refs = [vol.at[0, e] for e in range(3)]
    down_refs = [vol.at[1, e] for e in range(3)]

    around = []
    for e in range(3):
        z = jnp.concatenate([up_cells[e], own_cells[e], down_cells[e]], axis=0)
        around += [pltpu.roll(z, 2, 1), z, pltpu.roll(z, CW - 2, 1)]
    around.append(jnp.zeros((KE - 9 * VD, CW), BF16))
    h = jnp.dot(t_edge[...], jnp.concatenate(around, axis=0), preferred_element_type=F32)
    h = jnp.maximum(h + c1[0:HD, :], 0.0)
    lane = iota((HD, CW), 1)
    hrow = iota((HD, CW), 0) // C
    gone = (no_up & (hrow == 0)) | (no_down & (hrow == HR - 1))
    gone = gone | ((col == 0) & (lane % 2 == 1)) | ((col == cols_last) & (lane % 2 == 0))
    hcol = jnp.where(gone, 0.0, h).astype(BF16)

    pad = jnp.zeros((HD, CW), BF16)
    for e in range(3):
        hid[e, 0:HD, :] = pad
        hid[e, (D + 1) * HD : (D + 2) * HD, :] = pad

    hl = iota((C, CW), 1)
    hfirst = hl == 0
    hlast = hl == CW - 1

    def conv_one(j):
        d0 = j * 4
        top = jnp.dot(t_halo[0:128, :], window_rows(up_refs, j), preferred_element_type=F32)
        bottom = jnp.dot(t_halo[128:256, :], window_rows(down_refs, j), preferred_element_type=F32)
        for i in range(2):
            cut = slice(i * CW, (i + 1) * CW)
            for dd in range(2):
                d = d0 + 2 * i + dd
                border = pltpu.roll(hcol, (2 * CW - 1 - 2 * d) % CW, 1)
                for r in range(HR):
                    at = (r * 2 + dd) * C
                    halo = top if r < 2 else bottom
                    ha = at % 128
                    h = acc[j, at : at + C, cut] + halo[ha : ha + C, cut]
                    h = jnp.maximum(h, 0.0)
                    if r == 0:
                        h = jnp.where(no_up, 0.0, h)
                    if r == HR - 1:
                        h = jnp.where(no_down, 0.0, h)
                    h = h.astype(BF16)
                    b = border[r * C : (r + 1) * C]
                    base = (d + 1) * HD + r * C
                    hid[0, base : base + C, :] = jnp.where(hfirst, b, pltpu.roll(h, 1, 1))
                    hid[1, base : base + C, :] = h
                    hid[2, base : base + C, :] = jnp.where(hlast, b, pltpu.roll(h, CW - 1, 1))

    def hidden_rows(at, *more):
        return jnp.concatenate(
            [
                jnp.concatenate([hid[e, x * HD : x * HD + 256, :] for x in (at, *more)], axis=1)
                for e in range(3)
            ],
            axis=0,
        )

    ends = {}

    def conv_two(j):
        d0 = j * 8
        mid = jnp.dot(t_mid[...], hidden_rows(d0 + 2, d0 + 6), preferred_element_type=F32)
        both = jnp.dot(t_ends[...], hidden_rows(d0, d0 + 4), preferred_element_type=F32)
        ends[2 * j] = both[:, 0:CW]
        ends[2 * j + 1] = both[:, CW:]
        return mid

    def result(j, mid):
        d0 = j * 8
        parts = []
        for i in range(2):
            low = ends.pop(2 * j + i)
            high = ends[2 * j + i + 1]
            for p in range(8):
                at = p * C
                end = low[at : at + C] if p < 4 else high[at : at + C]
                v = own_vol[1, (d0 + 4 * i + 1) * OD + at : (d0 + 4 * i + 1) * OD + at + C, :]
                a = mid[at : at + C, i * CW : (i + 1) * CW] + end + c2[0:C, :] + v.astype(F32)
                parts.append(a)
        ready[j] = jnp.swapaxes(jnp.stack(parts, axis=0).astype(BF16), 0, 1)
        copy = pltpu.make_async_copy(ready.at[j], out_ref.at[:, pl.ds(j * 16, 16), :], sems.at[j])
        copy.start()
        return copy

    blocks([Rows(ups, up_cells, up_refs), Rows(downs, down_cells, down_refs)], conv_one)
    copies = []
    mid = conv_two(0)
    for j in range(1, D // 8):
        later = conv_two(j)
        copies.append(result(j - 1, mid))
        mid = later
    ends[D // 4] = jnp.dot(t_ends[...], hidden_rows(D), preferred_element_type=F32)
    copies.append(result(D // 8 - 1, mid))
    for copy in copies:
        copy.wait()


def aggregated(first, pair, cross, t_own, *ready):
    return pl.pallas_call(
        aggregate,
        out_shape=jax.ShapeDtypeStruct((C, D * RH, CW), BF16),
        in_specs=[VMEM] * 12,
        out_specs=pl.BlockSpec(memory_space=pl.ANY),
        scratch_shapes=[
            pltpu.VMEM((2, 3, (D + 2) * OD, CW), BF16),
            pltpu.VMEM((3, (D + 2) * HD, CW), BF16),
            pltpu.VMEM((D // 8, C, 16, CW), BF16),
            pltpu.SemaphoreType.DMA((D // 8,)),
        ],
        compiler_params=pltpu.CompilerParams(vmem_limit_bytes=32 * MIB),
        name="aggregate",
    )(*first, pair, cross, *ready)


def ring(x, axis, by):
    n = lax.axis_size(axis)
    return lax.ppermute(x, axis, [(i, (i + by) % n) for i in range(n)])


def swap(x, axis, first):
    n = lax.axis_size(axis)
    pairs = []
    for i in range(first, n + first, 2):
        a, b = i % n, (i + 1) % n
        pairs += [(a, b), (b, a)]
    return lax.ppermute(x, axis, pairs)


def body(left, right, offsets, weight_one, bias_one, weight_two, bias_two):
    lr = jnp.concatenate([left.reshape(C * RH, CW), right.reshape(C * RH, CW)], axis=0)
    x = packed(offsets, lr)
    xr = ring(x, "cols", -1)
    xl = ring(x, "cols", 1)
    x2 = ring(x, "cols", 2)
    x3 = ring(x, "cols", 3)
    x4 = ring(x, "cols", 4)
    ready = prepared(weight_one, weight_two, bias_one, bias_two)
    own = windows(offsets, xr, xl, x2, x3, x4, x, lr, ready[5])
    pair = swap(own, "rows", 0)
    cross = swap(own, "rows", 1)
    out = aggregated(begun(own, ready[0], ready[5], ready[7]), pair, cross, *ready)
    return out.reshape(C, D, RH, CW)


def solution(mesh):
    return jax.shard_map(
        body,
        mesh=mesh,
        in_specs=(P(None, "rows", "cols"), P(None, "rows", "cols"), P("cols"), P(), P(), P(), P()),
        out_specs=P(None, None, "rows", "cols"),
        check_vma=False,
    )
```

```python
import jax
import jax.numpy as jnp
from jax import lax
from jax.experimental import pallas as pl
from jax.experimental.pallas import tpu as pltpu
from jax.sharding import PartitionSpec as P

C = 32
D = 48
RH = 2
CW = 128
VR = RH + 4
HR = RH + 2
VD = VR * C
HD = HR * C
OD = RH * C
KK = 768
KE = 1792
F32 = jnp.float32
BF16 = jnp.bfloat16
MIB = 1024 * 1024
VMEM = pl.BlockSpec(memory_space=pltpu.VMEM)
SMEM = pl.BlockSpec(memory_space=pltpu.SMEM)


def iota(shape, dim):
    return lax.broadcasted_iota(jnp.int32, shape, dim)


def prepare(
    w_ref, b_ref, own_ref, halo_ref, edge_ref, mid_ref, ends_ref, c1_ref, c2_ref, sel_ref
):
    zero = jnp.zeros((C, C), F32)

    def taps(base):
        return {
            (a, b, e): w_ref[base + 9 * a + 3 * b + e].astype(F32)
            for a in range(3)
            for b in range(3)
            for e in range(3)
        }

    def fill(ref, row, parts):
        for q in range(0, len(parts), 4):
            ref[row : row + C, q * C : (q + 4) * C] = jnp.concatenate(
                parts[q : q + 4], axis=1
            ).astype(BF16)

    one = taps(0)
    for r in range(HR):
        for d in range(2):
            row = (r * 2 + d) * C

            def band(rows):
                return [
                    one.get((dl - d, rl - r, e), zero)
                    for e in range(3)
                    for dl in range(4)
                    for rl in rows
                ]

            fill(own_ref, row, band((2, 3)))
            fill(halo_ref, row, band((0, 1) if r < 2 else (4, 5)))
        fill(
            edge_ref,
            r * C,
            [
                one.get((a, rl - r, e), zero)
                for e in range(3)
                for a in range(3)
                for rl in range(VR)
            ]
            + [zero] * 2,
        )
    two = taps(27)
    for d in range(4):
        for h in range(RH):
            row = (d * RH + h) * C

            def band2(deep):
                return [
                    two.get((dl - d, rl - h, e), zero)
                    for e in range(3)
                    for dl in deep
                    for rl in range(HR)
                ]

            fill(mid_ref, row, band2((2, 3)))
            fill(ends_ref, row, band2((0, 1) if d < 2 else (4, 5)))
    eye = iota((C, C), 0) == iota((C, C), 1)

    def column(b):
        b = jnp.sum(jnp.where(eye, jnp.broadcast_to(b, (C, C)), 0.0), axis=1, keepdims=True)
        return jnp.broadcast_to(b, (C, CW))

    one, two = column(b_ref[0:1, :]), column(b_ref[1:2, :])
    for p in range(8):
        c1_ref[p * C : (p + 1) * C, :] = one
        c2_ref[p * C : (p + 1) * C, :] = two
    lane = iota((128, 128), 1)
    src = iota((128, 128), 0)
    d = lane // 2
    used = d < D
    left = (lane % 2 == 1) & used
    right = (lane % 2 == 0) & used
    right_of = (
        ((3, 47 - d), (2, 47 - d)),
        ((3, 48 - d), (3, 111 - d)),
        ((1, 48 - d), (3, 112 - d)),
    )
    left_of = (((3, 50), (0, 127)), ((3, 51), (3, 114)), ((0, 0), (3, 115)))
    for e in range(3):
        for which, table in ((0, right_of), (1, left_of)):
            for t in range(4):
                hit = jnp.zeros((128, 128), jnp.bool_)
                for mask, (tile, place) in zip((left, right), table[e]):
                    if tile == t:
                        hit = hit | (mask & (src == place))
                g = 2 * e + which
                sel_ref[t * 128 : (t + 1) * 128, g * 128 : (g + 1) * 128] = jnp.where(
                    hit, 1.0, 0.0
                ).astype(BF16)


def prepared(weight_one, weight_two, bias_one, bias_two):
    return pl.pallas_call(
        prepare,
        out_shape=(
            jax.ShapeDtypeStruct((256, KK), BF16),
            jax.ShapeDtypeStruct((256, KK), BF16),
            jax.ShapeDtypeStruct((HD, KE), BF16),
            jax.ShapeDtypeStruct((256, KK), BF16),
            jax.ShapeDtypeStruct((256, KK), BF16),
            jax.ShapeDtypeStruct((256, CW), F32),
            jax.ShapeDtypeStruct((256, CW), F32),
            jax.ShapeDtypeStruct((512, 768), BF16),
        ),
        in_specs=[VMEM] * 2,
        out_specs=[VMEM] * 8,
        cost_estimate=pl.CostEstimate(flops=1000000, bytes_accessed=4000000, transcendentals=0),
        compiler_params=pltpu.CompilerParams(vmem_limit_bytes=12 * MIB),
        name="prepare",
    )(jnp.concatenate([weight_one, weight_two], axis=0), jnp.stack([bias_one, bias_two]))


def pack(off_ref, lr_ref, out_ref):
    out_ref[0:64, :] = lr_ref[64:128, :]
    k = iota((16, CW), 0)
    at = iota((16, CW), 1)
    of_left = ((k < 2) & (at == k + 126)) | ((k >= 2) & (k < 4) & (at == k - 2))
    of_right = (k >= 4) & (k < 6) & (at == k - 4)

    def columns(chosen, rows):
        return lax.dot_general(
            jnp.where(chosen, 1.0, 0.0).astype(BF16),
            rows,
            (((1,), (1,)), ((), ())),
            preferred_element_type=F32,
        )

    edge = columns(of_left, lr_ref[0:64, :]) + columns(of_right, lr_ref[64:128, :])
    o = off_ref[0]
    code = jnp.where(k == 6, o // 8, jnp.where(k == 7, o % 8, 0)).astype(F32)
    edge = jnp.concatenate([edge, jnp.zeros((16, 64), F32)], axis=1) + code
    out_ref[64:80, :] = edge.astype(BF16)


def packed(offsets, lr):
    return pl.pallas_call(
        pack,
        out_shape=jax.ShapeDtypeStruct((80, CW), BF16),
        in_specs=[SMEM, VMEM],
        out_specs=VMEM,
        compiler_params=pltpu.CompilerParams(vmem_limit_bytes=2 * MIB),
        name="pack",
    )(offsets, lr)


def cut(off_ref, even_ref, odd_ref, x2, x3, x4, xo, lr_ref, after_ref, out_ref, tiles):
    col = lax.axis_index("cols")
    final = lax.axis_size("cols") - 1
    o = off_ref[0]
    even, odd = even_ref[...], odd_ref[...]
    second = col % 2 == 1
    xl = jnp.where(second, even, odd)
    xr = jnp.where(second, odd, even)

    def scalar_of(ref):
        v = ref[64:80].astype(F32)
        return jnp.max(v[6:7, 64:128] * 8.0 + v[7:8, 64:128]).astype(jnp.int32)

    o_l = scalar_of(xl)
    o_r = scalar_of(xr)
    dst = iota((64, 64), 0)
    src = iota((64, 64), 1)
    perm = jnp.where(src == (dst % C) * RH + dst // C, 1.0, 0.0).astype(BF16)
    k = iota((16, CW), 0)
    at = iota((16, CW), 1)

    def rows(x):
        return jnp.dot(perm, x, preferred_element_type=F32)

    def placed(ref, chosen):
        edge = lax.dot_general(
            ref[64:80, 0:64],
            jnp.where(chosen, 1.0, 0.0).astype(BF16),
            (((0,), (0,)), ((), ())),
            preferred_element_type=F32,
        )
        return rows(edge.astype(BF16))

    for t, x in enumerate((x4, x3, x2, xl, xo)):
        keep = (col + (t - 4) >= 0).astype(F32)
        tiles[t] = rows(x[0:64, :]) * keep
    tiles[5] = placed(xr, (k >= 4) & (k < 6) & (at == k - 4))
    lane = iota((64, CW), 1)

    def window(start):
        t = start // CW
        s = start % CW
        back = (CW - s) % CW
        a = tiles[t]
        b = tiles[t + 1]
        return t, s, back, pltpu.roll(jnp.where(lane < s, b, a), back, 1)

    t, s, back, one = window(464 - o)
    two = pltpu.roll(jnp.where(lane < s, tiles[t + 2], tiles[t + 1]), back, 1)
    wl = window(463 - o_l)[3]
    wr = window(529 - o_r)[3]
    near = placed(xl, (k < 2) & (at == k + 50)) * (col > 0).astype(F32)
    far = placed(xr, (k >= 2) & (k < 4) & (at == k + 112)) * (col < final).astype(F32)
    border = jnp.where(lane < 50, wl, jnp.where(lane < 64, near, jnp.where(lane < 114, wr, far)))
    out_ref[0:64, :] = rows(lr_ref[0:64, :]).astype(BF16)
    out_ref[64:128, :] = one.astype(BF16)
    out_ref[128:192, :] = two.astype(BF16)
    out_ref[192:256, :] = border.astype(BF16)


def windows(offsets, even, odd, x2, x3, x4, xo, lr, after):
    return pl.pallas_call(
        cut,
        out_shape=jax.ShapeDtypeStruct((256, CW), BF16),
        in_specs=[SMEM] + [VMEM] * 7 + [pl.BlockSpec(memory_space=pl.ANY)],
        out_specs=VMEM,
        scratch_shapes=[pltpu.VMEM((6, 64, CW), F32)],
        compiler_params=pltpu.CompilerParams(vmem_limit_bytes=4 * MIB),
        name="windows",
    )(offsets, even, odd, x2, x3, x4, xo, lr, after)


def border_cells(tiles, sel):
    picked = jnp.dot(jnp.concatenate(tiles, axis=1), sel, preferred_element_type=F32)
    cells = []
    for e in range(3):
        r = picked[:, (2 * e) * CW : (2 * e + 1) * CW]
        lft = picked[:, (2 * e + 1) * CW : (2 * e + 2) * CW]
        cells.append((r * lft).astype(BF16))
    return cells


class Rows:
    def __init__(self, tiles, cells, refs):
        left, self.win0, self.win1, _ = tiles
        self.l0, self.l1, self.l2 = pltpu.roll(left, 1, 1), left, pltpu.roll(left, CW - 1, 1)
        self.z = cells[1]
        self.refs = refs
        self.lane = iota((OD, CW), 1)
        pad = jnp.zeros((OD, CW), BF16)
        for ref in refs:
            ref[0:OD, :] = pad
            ref[(D + 1) * OD : (D + 2) * OD, :] = pad
        self.held = {k: self.shifted(k) for k in (D, D + 1)}

    def shifted(self, k):
        if k == 0:
            return self.win0
        return pltpu.roll(jnp.where(self.lane < k, self.win1, self.win0), CW - k, 1)

    def disparity(self, d):
        k = D - 1 - d
        base = (d + 1) * OD
        self.held[k] = self.shifted(k)
        border = pltpu.roll(self.z, (2 * CW - 1 - 2 * d) % CW, 1)
        before, here, after = self.refs
        before[base : base + OD, :] = jnp.where(self.lane == 0, border, self.l0 * self.held[k])
        here[base : base + OD, :] = self.l1 * self.held[k + 1]
        after[base : base + OD, :] = jnp.where(
            self.lane == CW - 1, border, self.l2 * self.held.pop(k + 2)
        )


def window_rows(refs, j):
    d0 = j * 4
    return jnp.concatenate(
        [
            jnp.concatenate(
                [ref[d0 * OD : d0 * OD + 256, :], ref[(d0 + 2) * OD : (d0 + 2) * OD + 256, :]], axis=1
            )
            for ref in refs
        ],
        axis=0,
    )


def blocks(groups, conv):
    done = 0
    for j in range(D // 4):
        upto = min(D, 4 * j + 5)
        for d in range(done, upto):
            for g in groups:
                g.disparity(d)
        done = upto
        conv(j)


def begin(own, t_own, c1, sel, vol_ref, cells_ref, acc_ref):
    tiles = [own[t * 64 : t * 64 + 64, :] for t in range(4)]
    cells = border_cells(tiles, sel[...])
    for e in range(3):
        cells_ref[e] = cells[e]
    refs = [vol_ref.at[e] for e in range(3)]

    def conv(j):
        y = jnp.dot(t_own[...], window_rows(refs, j), preferred_element_type=F32)
        acc_ref[j] = y + jnp.concatenate([c1[...], c1[...]], axis=1)

    blocks([Rows(tiles, cells, refs)], conv)


def begun(own, t_own, c1, sel):
    return pl.pallas_call(
        begin,
        out_shape=(
            jax.ShapeDtypeStruct((3, (D + 2) * OD, CW), BF16),
            jax.ShapeDtypeStruct((3, OD, CW), BF16),
            jax.ShapeDtypeStruct((D // 4, 256, 256), F32),
        ),
        in_specs=[VMEM] * 4,
        out_specs=[VMEM] * 3,
        cost_estimate=pl.CostEstimate(
            flops=2 * 12 * 256 * 768 * 256, bytes_accessed=6000000, transcendentals=0
        ),
        compiler_params=pltpu.CompilerParams(vmem_limit_bytes=12 * MIB),
        name="begin",
    )(own, t_own, c1, sel)


def aggregate(
    own_vol,
    own_cells,
    acc,
    pair,
    cross,
    t_halo,
    t_edge,
    t_mid,
    t_ends,
    c1,
    c2,
    sel,
    out_ref,
    vol,
    hid,
    ready,
    sems,
):
    row = lax.axis_index("rows")
    col = lax.axis_index("cols")
    rows_last = lax.axis_size("rows") - 1
    cols_last = lax.axis_size("cols") - 1
    odd = row % 2 == 1
    no_up = row == 0
    no_down = row == rows_last
    keep_up = 1.0 - no_up.astype(F32)
    keep_down = 1.0 - no_down.astype(F32)

    def tile(t):
        part = slice(t * 64, t * 64 + 64)
        p = pair[part, :]
        x = cross[part, :]
        up = jnp.where(odd, p, x)
        down = jnp.where(odd, x, p)
        up = jnp.where(no_up, jnp.zeros_like(up), up)
        down = jnp.where(no_down, jnp.zeros_like(down), down)
        return up, down

    ups, downs = zip(*(tile(t) for t in range(4)))
    halo_cells = border_cells(
        [jnp.concatenate([u, w], axis=0) for u, w in zip(ups, downs)], sel[...]
    )
    up_cells = [z[0:OD] for z in halo_cells]
    down_cells = [z[OD:] for z in halo_cells]
    up_refs = [vol.at[0, e] for e in range(3)]
    down_refs = [vol.at[1, e] for e in range(3)]

    around = []
    for e in range(3):
        z = jnp.concatenate([up_cells[e], own_cells[e], down_cells[e]], axis=0)
        around += [pltpu.roll(z, 2, 1), z, pltpu.roll(z, CW - 2, 1)]
    around.append(jnp.zeros((KE - 9 * VD, CW), BF16))
    h = jnp.dot(t_edge[...], jnp.concatenate(around, axis=0), preferred_element_type=F32)
    h = jnp.maximum(h + c1[0:HD, :], 0.0)
    lane = iota((HD, CW), 1)
    hrow = iota((HD, CW), 0) // C
    gone = (no_up & (hrow == 0)) | (no_down & (hrow == HR - 1))
    gone = gone | ((col == 0) & (lane % 2 == 1)) | ((col == cols_last) & (lane % 2 == 0))
    hcol = jnp.where(gone, 0.0, h).astype(BF16)

    pad = jnp.zeros((HD, CW), BF16)
    for e in range(3):
        hid[e, 0:HD, :] = pad
        hid[e, (D + 1) * HD : (D + 2) * HD, :] = pad

    hl = iota((C, CW), 1)
    hfirst = hl == 0
    hlast = hl == CW - 1

    def conv_one(j):
        d0 = j * 4
        top = jnp.dot(t_halo[0:128, :], window_rows(up_refs, j), preferred_element_type=F32)
        bottom = jnp.dot(t_halo[128:256, :], window_rows(down_refs, j), preferred_element_type=F32)
        for i in range(2):
            cut = slice(i * CW, (i + 1) * CW)
            for dd in range(2):
                d = d0 + 2 * i + dd
                border = pltpu.roll(hcol, (2 * CW - 1 - 2 * d) % CW, 1)
                for r in range(HR):
                    at = (r * 2 + dd) * C
                    halo = top if r < 2 else bottom
                    ha = at % 128
                    h = acc[j, at : at + C, cut] + halo[ha : ha + C, cut]
                    h = jnp.maximum(h, 0.0)
                    if r == 0:
                        h = h * keep_up
                    if r == HR - 1:
                        h = h * keep_down
                    h = h.astype(BF16)
                    b = border[r * C : (r + 1) * C]
                    base = (d + 1) * HD + r * C
                    hid[0, base : base + C, :] = jnp.where(hfirst, b, pltpu.roll(h, 1, 1))
                    hid[1, base : base + C, :] = h
                    hid[2, base : base + C, :] = jnp.where(hlast, b, pltpu.roll(h, CW - 1, 1))

    def hidden_rows(at, *more):
        return jnp.concatenate(
            [
                jnp.concatenate([hid[e, x * HD : x * HD + 256, :] for x in (at, *more)], axis=1)
                for e in range(3)
            ],
            axis=0,
        )

    ends = {}

    def conv_two(j):
        d0 = j * 8
        mid = jnp.dot(t_mid[...], hidden_rows(d0 + 2, d0 + 6), preferred_element_type=F32)
        both = jnp.dot(t_ends[...], hidden_rows(d0, d0 + 4), preferred_element_type=F32)
        ends[2 * j] = both[:, 0:CW]
        ends[2 * j + 1] = both[:, CW:]
        return mid

    def result(j, mid):
        d0 = j * 8
        parts = []
        for i in range(2):
            low = ends.pop(2 * j + i)
            high = ends[2 * j + i + 1]
            for p in range(8):
                at = p * C
                end = low[at : at + C] if p < 4 else high[at : at + C]
                v = own_vol[1, (d0 + 4 * i + 1) * OD + at : (d0 + 4 * i + 1) * OD + at + C, :]
                a = mid[at : at + C, i * CW : (i + 1) * CW] + end + c2[0:C, :] + v.astype(F32)
                parts.append(a)
        ready[j] = jnp.swapaxes(jnp.stack(parts, axis=0).astype(BF16), 0, 1)
        copy = pltpu.make_async_copy(ready.at[j], out_ref.at[:, pl.ds(j * 16, 16), :], sems.at[j])
        copy.start()
        return copy

    blocks([Rows(ups, up_cells, up_refs), Rows(downs, down_cells, down_refs)], conv_one)
    copies = []
    mid = conv_two(0)
    for j in range(1, D // 8):
        later = conv_two(j)
        copies.append(result(j - 1, mid))
        mid = later
    ends[D // 4] = jnp.dot(t_ends[...], hidden_rows(D), preferred_element_type=F32)
    copies.append(result(D // 8 - 1, mid))
    for copy in copies:
        copy.wait()


def aggregated(first, pair, cross, t_own, *ready):
    return pl.pallas_call(
        aggregate,
        out_shape=jax.ShapeDtypeStruct((C, D * RH, CW), BF16),
        in_specs=[VMEM] * 12,
        out_specs=pl.BlockSpec(memory_space=pl.ANY),
        scratch_shapes=[
            pltpu.VMEM((2, 3, (D + 2) * OD, CW), BF16),
            pltpu.VMEM((3, (D + 2) * HD, CW), BF16),
            pltpu.VMEM((D // 8, C, 16, CW), BF16),
            pltpu.SemaphoreType.DMA((D // 8,)),
        ],
        compiler_params=pltpu.CompilerParams(vmem_limit_bytes=32 * MIB),
        name="aggregate",
    )(*first, pair, cross, *ready)


def ahead(x, by):
    n = lax.axis_size("cols")
    return lax.ppermute(x, "cols", [(i, i + by if i + by < n else n - 1 - i) for i in range(n)])


def swap(x, axis, first):
    n = lax.axis_size(axis)
    pairs = []
    for i in range(first, n + first, 2):
        a, b = i % n, (i + 1) % n
        pairs += [(a, b), (b, a)]
    return lax.ppermute(x, axis, pairs)


def swap_inner(x):
    rows, cols = lax.axis_size("rows"), lax.axis_size("cols")
    pairs = []
    for r in range(rows):
        near = r ^ 1 if (r ^ 1) < rows else r
        for c in range(cols):
            if c in (0, cols - 1):
                to = near * cols + c
            else:
                to = r * cols + (c + 1 if c % 2 else c - 1)
            pairs.append((r * cols + c, to))
    return lax.ppermute(x, ("rows", "cols"), pairs)


def body(left, right, offsets, weight_one, bias_one, weight_two, bias_two):
    lr = jnp.concatenate([left.reshape(C * RH, CW), right.reshape(C * RH, CW)], axis=0)
    x = packed(offsets, lr)
    even = swap(x, "cols", 0)
    odd = swap_inner(x)
    x2 = ahead(x, 2)
    x3 = ahead(x, 3)
    x4 = ahead(x, 4)
    ready = prepared(weight_one, weight_two, bias_one, bias_two)
    own = windows(offsets, even, odd, x2, x3, x4, x, lr, ready[5])
    pair = swap(own, "rows", 0)
    cross = swap(own, "rows", 1)
    out = aggregated(begun(own, ready[0], ready[5], ready[7]), pair, cross, *ready)
    return out.reshape(C, D, RH, CW)


def solution(mesh):
    return jax.shard_map(
        body,
        mesh=mesh,
        in_specs=(P(None, "rows", "cols"), P(None, "rows", "cols"), P("cols"), P(), P(), P(), P()),
        out_specs=P(None, None, "rows", "cols"),
        check_vma=False,
    )
```

```python
import jax
import jax.numpy as jnp
from jax import lax
from jax.experimental import pallas as pl
from jax.experimental.pallas import tpu as pltpu
from jax.sharding import PartitionSpec as P

C = 32
D = 48
RH = 2
CW = 128
VR = RH + 4
HR = RH + 2
VD = VR * C
HD = HR * C
OD = RH * C
KK = 768
KE = 1792
F32 = jnp.float32
BF16 = jnp.bfloat16
MIB = 1024 * 1024
VMEM = pl.BlockSpec(memory_space=pltpu.VMEM)
SMEM = pl.BlockSpec(memory_space=pltpu.SMEM)


def iota(shape, dim):
    return lax.broadcasted_iota(jnp.int32, shape, dim)


def prepare(
    w_ref, b_ref, own_ref, halo_ref, edge_ref, mid_ref, ends_ref, c1_ref, c2_ref, sel_ref
):
    zero = jnp.zeros((C, C), F32)

    def taps(base):
        return {
            (a, b, e): w_ref[base + 9 * a + 3 * b + e].astype(F32)
            for a in range(3)
            for b in range(3)
            for e in range(3)
        }

    def fill(ref, row, parts):
        for q in range(0, len(parts), 4):
            ref[row : row + C, q * C : (q + 4) * C] = jnp.concatenate(
                parts[q : q + 4], axis=1
            ).astype(BF16)

    one = taps(0)
    for r in range(HR):
        for d in range(2):
            row = (r * 2 + d) * C

            def band(rows):
                return [
                    one.get((dl - d, rl - r, e), zero)
                    for e in range(3)
                    for dl in range(4)
                    for rl in rows
                ]

            fill(own_ref, row, band((2, 3)))
            fill(halo_ref, row, band((0, 1) if r < 2 else (4, 5)))
        fill(
            edge_ref,
            r * C,
            [
                one.get((a, rl - r, e), zero)
                for e in range(3)
                for a in range(3)
                for rl in range(VR)
            ]
            + [zero] * 2,
        )
    two = taps(27)
    for d in range(4):
        for h in range(RH):
            row = (d * RH + h) * C

            def band2(deep):
                return [
                    two.get((dl - d, rl - h, e), zero)
                    for e in range(3)
                    for dl in deep
                    for rl in range(HR)
                ]

            fill(mid_ref, row, band2((2, 3)))
            fill(ends_ref, row, band2((0, 1) if d < 2 else (4, 5)))
    eye = iota((C, C), 0) == iota((C, C), 1)

    def column(b):
        b = jnp.sum(jnp.where(eye, jnp.broadcast_to(b, (C, C)), 0.0), axis=1, keepdims=True)
        return jnp.broadcast_to(b, (C, CW))

    one, two = column(b_ref[0:1, :]), column(b_ref[1:2, :])
    for p in range(8):
        c1_ref[p * C : (p + 1) * C, :] = one
        c2_ref[p * C : (p + 1) * C, :] = two
    lane = iota((128, 128), 1)
    src = iota((128, 128), 0)
    d = lane // 2
    used = d < D
    left = (lane % 2 == 1) & used
    right = (lane % 2 == 0) & used
    right_of = (
        ((3, 47 - d), (2, 47 - d)),
        ((3, 48 - d), (3, 111 - d)),
        ((1, 48 - d), (3, 112 - d)),
    )
    left_of = (((3, 50), (0, 127)), ((3, 51), (3, 114)), ((0, 0), (3, 115)))
    for e in range(3):
        for which, table in ((0, right_of), (1, left_of)):
            for t in range(4):
                hit = jnp.zeros((128, 128), jnp.bool_)
                for mask, (tile, place) in zip((left, right), table[e]):
                    if tile == t:
                        hit = hit | (mask & (src == place))
                g = 2 * e + which
                sel_ref[t * 128 : (t + 1) * 128, g * 128 : (g + 1) * 128] = jnp.where(
                    hit, 1.0, 0.0
                ).astype(BF16)


def prepared(weight_one, weight_two, bias_one, bias_two):
    return pl.pallas_call(
        prepare,
        out_shape=(
            jax.ShapeDtypeStruct((256, KK), BF16),
            jax.ShapeDtypeStruct((256, KK), BF16),
            jax.ShapeDtypeStruct((HD, KE), BF16),
            jax.ShapeDtypeStruct((256, KK), BF16),
            jax.ShapeDtypeStruct((256, KK), BF16),
            jax.ShapeDtypeStruct((256, CW), F32),
            jax.ShapeDtypeStruct((256, CW), F32),
            jax.ShapeDtypeStruct((512, 768), BF16),
        ),
        in_specs=[VMEM] * 2,
        out_specs=[VMEM] * 8,
        cost_estimate=pl.CostEstimate(flops=0, bytes_accessed=0, transcendentals=0),
        compiler_params=pltpu.CompilerParams(vmem_limit_bytes=12 * MIB),
        name="prepare",
    )(jnp.concatenate([weight_one, weight_two], axis=0), jnp.stack([bias_one, bias_two]))


def pack(off_ref, lr_ref, out_ref):
    out_ref[0:64, :] = lr_ref[64:128, :]
    k = iota((16, CW), 0)
    at = iota((16, CW), 1)
    of_left = ((k < 2) & (at == k + 126)) | ((k >= 2) & (k < 4) & (at == k - 2))
    of_right = (k >= 4) & (k < 6) & (at == k - 4)

    def columns(chosen, rows):
        return lax.dot_general(
            jnp.where(chosen, 1.0, 0.0).astype(BF16),
            rows,
            (((1,), (1,)), ((), ())),
            preferred_element_type=F32,
        )

    edge = columns(of_left, lr_ref[0:64, :]) + columns(of_right, lr_ref[64:128, :])
    o = off_ref[0]
    code = jnp.where(k == 6, o // 8, jnp.where(k == 7, o % 8, 0)).astype(F32)
    edge = jnp.concatenate([edge, jnp.zeros((16, 64), F32)], axis=1) + code
    out_ref[64:80, :] = edge.astype(BF16)


def packed(offsets, lr):
    return pl.pallas_call(
        pack,
        out_shape=jax.ShapeDtypeStruct((80, CW), BF16),
        in_specs=[SMEM, VMEM],
        out_specs=VMEM,
        compiler_params=pltpu.CompilerParams(vmem_limit_bytes=2 * MIB),
        name="pack",
    )(offsets, lr)


def cut(off_ref, even_ref, odd_ref, x2, x3, x4, xo, lr_ref, after_ref, out_ref, tiles):
    col = lax.axis_index("cols")
    final = lax.axis_size("cols") - 1
    o = off_ref[0]
    even, odd = even_ref[...], odd_ref[...]
    second = col % 2 == 1
    xl = jnp.where(second, even, odd)
    xr = jnp.where(second, odd, even)

    def scalar_of(ref):
        v = ref[64:80].astype(F32)
        return jnp.max(v[6:7, 64:128] * 8.0 + v[7:8, 64:128]).astype(jnp.int32)

    o_l = scalar_of(xl)
    o_r = scalar_of(xr)
    dst = iota((64, 64), 0)
    src = iota((64, 64), 1)
    perm = jnp.where(src == (dst % C) * RH + dst // C, 1.0, 0.0).astype(BF16)
    k = iota((16, CW), 0)
    at = iota((16, CW), 1)

    def rows(x):
        return jnp.dot(perm, x, preferred_element_type=F32)

    def placed(ref, chosen):
        edge = lax.dot_general(
            ref[64:80, 0:64],
            jnp.where(chosen, 1.0, 0.0).astype(BF16),
            (((0,), (0,)), ((), ())),
            preferred_element_type=F32,
        )
        return rows(edge.astype(BF16))

    for t, x in enumerate((x4, x3, x2, xl, xo)):
        keep = (col + (t - 4) >= 0).astype(F32)
        tiles[t] = rows(x[0:64, :]) * keep
    tiles[5] = placed(xr, (k >= 4) & (k < 6) & (at == k - 4))
    lane = iota((64, CW), 1)

    def window(start):
        t = start // CW
        s = start % CW
        back = (CW - s) % CW
        a = tiles[t]
        b = tiles[t + 1]
        return t, s, back, pltpu.roll(jnp.where(lane < s, b, a), back, 1)

    t, s, back, one = window(464 - o)
    two = pltpu.roll(jnp.where(lane < s, tiles[t + 2], tiles[t + 1]), back, 1)
    wl = window(463 - o_l)[3]
    wr = window(529 - o_r)[3]
    near = placed(xl, (k < 2) & (at == k + 50)) * (col > 0).astype(F32)
    far = placed(xr, (k >= 2) & (k < 4) & (at == k + 112)) * (col < final).astype(F32)
    border = jnp.where(lane < 50, wl, jnp.where(lane < 64, near, jnp.where(lane < 114, wr, far)))
    out_ref[0:64, :] = rows(lr_ref[0:64, :]).astype(BF16)
    out_ref[64:128, :] = one.astype(BF16)
    out_ref[128:192, :] = two.astype(BF16)
    out_ref[192:256, :] = border.astype(BF16)


def windows(offsets, even, odd, x2, x3, x4, xo, lr, after):
    return pl.pallas_call(
        cut,
        out_shape=jax.ShapeDtypeStruct((256, CW), BF16),
        in_specs=[SMEM] + [VMEM] * 7 + [pl.BlockSpec(memory_space=pl.ANY)],
        out_specs=VMEM,
        scratch_shapes=[pltpu.VMEM((6, 64, CW), F32)],
        compiler_params=pltpu.CompilerParams(vmem_limit_bytes=4 * MIB),
        name="windows",
    )(offsets, even, odd, x2, x3, x4, xo, lr, after)


def border_cells(tiles, sel):
    picked = jnp.dot(jnp.concatenate(tiles, axis=1), sel, preferred_element_type=F32)
    cells = []
    for e in range(3):
        r = picked[:, (2 * e) * CW : (2 * e + 1) * CW]
        lft = picked[:, (2 * e + 1) * CW : (2 * e + 2) * CW]
        cells.append((r * lft).astype(BF16))
    return cells


class Rows:
    def __init__(self, tiles, cells, refs):
        left, self.win0, self.win1, _ = tiles
        self.l0, self.l1, self.l2 = pltpu.roll(left, 1, 1), left, pltpu.roll(left, CW - 1, 1)
        self.z = cells[1]
        self.refs = refs
        self.lane = iota((OD, CW), 1)
        pad = jnp.zeros((OD, CW), BF16)
        for ref in refs:
            ref[0:OD, :] = pad
            ref[(D + 1) * OD : (D + 2) * OD, :] = pad
        self.held = {k: self.shifted(k) for k in (D, D + 1)}

    def shifted(self, k):
        if k == 0:
            return self.win0
        return pltpu.roll(jnp.where(self.lane < k, self.win1, self.win0), CW - k, 1)

    def disparity(self, d):
        k = D - 1 - d
        base = (d + 1) * OD
        self.held[k] = self.shifted(k)
        border = pltpu.roll(self.z, (2 * CW - 1 - 2 * d) % CW, 1)
        before, here, after = self.refs
        before[base : base + OD, :] = jnp.where(self.lane == 0, border, self.l0 * self.held[k])
        here[base : base + OD, :] = self.l1 * self.held[k + 1]
        after[base : base + OD, :] = jnp.where(
            self.lane == CW - 1, border, self.l2 * self.held.pop(k + 2)
        )


def window_rows(refs, j):
    d0 = j * 4
    return jnp.concatenate(
        [
            jnp.concatenate(
                [ref[d0 * OD : d0 * OD + 256, :], ref[(d0 + 2) * OD : (d0 + 2) * OD + 256, :]], axis=1
            )
            for ref in refs
        ],
        axis=0,
    )


def blocks(groups, conv):
    done = 0
    for j in range(D // 4):
        upto = min(D, 4 * j + 5)
        for d in range(done, upto):
            for g in groups:
                g.disparity(d)
        done = upto
        conv(j)


def begin(own, t_own, c1, sel, vol_ref, cells_ref, acc_ref):
    tiles = [own[t * 64 : t * 64 + 64, :] for t in range(4)]
    cells = border_cells(tiles, sel[...])
    for e in range(3):
        cells_ref[e] = cells[e]
    refs = [vol_ref.at[e] for e in range(3)]

    def conv(j):
        y = jnp.dot(t_own[...], window_rows(refs, j), preferred_element_type=F32)
        acc_ref[j] = y + jnp.concatenate([c1[...], c1[...]], axis=1)

    blocks([Rows(tiles, cells, refs)], conv)


def begun(own, t_own, c1, sel):
    return pl.pallas_call(
        begin,
        out_shape=(
            jax.ShapeDtypeStruct((3, (D + 2) * OD, CW), BF16),
            jax.ShapeDtypeStruct((3, OD, CW), BF16),
            jax.ShapeDtypeStruct((D // 4, 256, 256), F32),
        ),
        in_specs=[VMEM] * 4,
        out_specs=[VMEM] * 3,
        cost_estimate=pl.CostEstimate(
            flops=2 * 12 * 256 * 768 * 256, bytes_accessed=6000000, transcendentals=0
        ),
        compiler_params=pltpu.CompilerParams(vmem_limit_bytes=12 * MIB),
        name="begin",
    )(own, t_own, c1, sel)


def aggregate(
    own_vol,
    own_cells,
    acc,
    pair,
    cross,
    t_halo,
    t_edge,
    t_mid,
    t_ends,
    c1,
    c2,
    sel,
    out_ref,
    vol,
    hid,
    ready,
    sems,
):
    row = lax.axis_index("rows")
    col = lax.axis_index("cols")
    rows_last = lax.axis_size("rows") - 1
    cols_last = lax.axis_size("cols") - 1
    odd = row % 2 == 1
    no_up = row == 0
    no_down = row == rows_last
    keep_up = 1.0 - no_up.astype(F32)
    keep_down = 1.0 - no_down.astype(F32)

    def tile(t):
        part = slice(t * 64, t * 64 + 64)
        p = pair[part, :]
        x = cross[part, :]
        up = jnp.where(odd, p, x)
        down = jnp.where(odd, x, p)
        up = jnp.where(no_up, jnp.zeros_like(up), up)
        down = jnp.where(no_down, jnp.zeros_like(down), down)
        return up, down

    ups, downs = zip(*(tile(t) for t in range(4)))
    halo_cells = border_cells(
        [jnp.concatenate([u, w], axis=0) for u, w in zip(ups, downs)], sel[...]
    )
    up_cells = [z[0:OD] for z in halo_cells]
    down_cells = [z[OD:] for z in halo_cells]
    up_refs = [vol.at[0, e] for e in range(3)]
    down_refs = [vol.at[1, e] for e in range(3)]

    around = []
    for e in range(3):
        z = jnp.concatenate([up_cells[e], own_cells[e], down_cells[e]], axis=0)
        around += [pltpu.roll(z, 2, 1), z, pltpu.roll(z, CW - 2, 1)]
    around.append(jnp.zeros((KE - 9 * VD, CW), BF16))
    h = jnp.dot(t_edge[...], jnp.concatenate(around, axis=0), preferred_element_type=F32)
    h = jnp.maximum(h + c1[0:HD, :], 0.0)
    lane = iota((HD, CW), 1)
    hrow = iota((HD, CW), 0) // C
    gone = (no_up & (hrow == 0)) | (no_down & (hrow == HR - 1))
    gone = gone | ((col == 0) & (lane % 2 == 1)) | ((col == cols_last) & (lane % 2 == 0))
    hcol = jnp.where(gone, 0.0, h).astype(BF16)

    pad = jnp.zeros((HD, CW), BF16)
    for e in range(3):
        hid[e, 0:HD, :] = pad
        hid[e, (D + 1) * HD : (D + 2) * HD, :] = pad

    hl = iota((C, CW), 1)
    hfirst = hl == 0
    hlast = hl == CW - 1

    def conv_one(j):
        d0 = j * 4
        top = jnp.dot(t_halo[0:128, :], window_rows(up_refs, j), preferred_element_type=F32)
        bottom = jnp.dot(t_halo[128:256, :], window_rows(down_refs, j), preferred_element_type=F32)
        for i in range(2):
            cut = slice(i * CW, (i + 1) * CW)
            for dd in range(2):
                d = d0 + 2 * i + dd
                border = pltpu.roll(hcol, (2 * CW - 1 - 2 * d) % CW, 1)
                for r in range(HR):
                    at = (r * 2 + dd) * C
                    halo = top if r < 2 else bottom
                    ha = at % 128
                    h = acc[j, at : at + C, cut] + halo[ha : ha + C, cut]
                    h = jnp.maximum(h, 0.0)
                    if r == 0:
                        h = h * keep_up
                    if r == HR - 1:
                        h = h * keep_down
                    h = h.astype(BF16)
                    b = border[r * C : (r + 1) * C]
                    base = (d + 1) * HD + r * C
                    hid[0, base : base + C, :] = jnp.where(hfirst, b, pltpu.roll(h, 1, 1))
                    hid[1, base : base + C, :] = h
                    hid[2, base : base + C, :] = jnp.where(hlast, b, pltpu.roll(h, CW - 1, 1))

    def hidden_rows(at, *more):
        return jnp.concatenate(
            [
                jnp.concatenate([hid[e, x * HD : x * HD + 256, :] for x in (at, *more)], axis=1)
                for e in range(3)
            ],
            axis=0,
        )

    ends = {}

    def conv_two(j):
        d0 = j * 8
        mid = jnp.dot(t_mid[...], hidden_rows(d0 + 2, d0 + 6), preferred_element_type=F32)
        both = jnp.dot(t_ends[...], hidden_rows(d0, d0 + 4), preferred_element_type=F32)
        ends[2 * j] = both[:, 0:CW]
        ends[2 * j + 1] = both[:, CW:]
        return mid

    def result(j, mid):
        d0 = j * 8
        parts = []
        for i in range(2):
            low = ends.pop(2 * j + i)
            high = ends[2 * j + i + 1]
            for p in range(8):
                at = p * C
                end = low[at : at + C] if p < 4 else high[at : at + C]
                v = own_vol[1, (d0 + 4 * i + 1) * OD + at : (d0 + 4 * i + 1) * OD + at + C, :]
                a = mid[at : at + C, i * CW : (i + 1) * CW] + end + c2[0:C, :] + v.astype(F32)
                parts.append(a)
        ready[j] = jnp.swapaxes(jnp.stack(parts, axis=0).astype(BF16), 0, 1)
        copy = pltpu.make_async_copy(ready.at[j], out_ref.at[:, pl.ds(j * 16, 16), :], sems.at[j])
        copy.start()
        return copy

    blocks([Rows(ups, up_cells, up_refs), Rows(downs, down_cells, down_refs)], conv_one)
    copies = []
    mid = conv_two(0)
    for j in range(1, D // 8):
        later = conv_two(j)
        copies.append(result(j - 1, mid))
        mid = later
    ends[D // 4] = jnp.dot(t_ends[...], hidden_rows(D), preferred_element_type=F32)
    copies.append(result(D // 8 - 1, mid))
    for copy in copies:
        copy.wait()


def aggregated(first, pair, cross, t_own, *ready):
    return pl.pallas_call(
        aggregate,
        out_shape=jax.ShapeDtypeStruct((C, D * RH, CW), BF16),
        in_specs=[VMEM] * 12,
        out_specs=pl.BlockSpec(memory_space=pl.ANY),
        scratch_shapes=[
            pltpu.VMEM((2, 3, (D + 2) * OD, CW), BF16),
            pltpu.VMEM((3, (D + 2) * HD, CW), BF16),
            pltpu.VMEM((D // 8, C, 16, CW), BF16),
            pltpu.SemaphoreType.DMA((D // 8,)),
        ],
        compiler_params=pltpu.CompilerParams(vmem_limit_bytes=32 * MIB),
        name="aggregate",
    )(*first, pair, cross, *ready)


def ahead(x, by):
    n = lax.axis_size("cols")
    return lax.ppermute(x, "cols", [(i, i + by if i + by < n else n - 1 - i) for i in range(n)])


def swap(x, axis, first):
    n = lax.axis_size(axis)
    pairs = []
    for i in range(first, n + first, 2):
        a, b = i % n, (i + 1) % n
        pairs += [(a, b), (b, a)]
    return lax.ppermute(x, axis, pairs)


def swap_inner(x):
    rows, cols = lax.axis_size("rows"), lax.axis_size("cols")
    pairs = []
    for r in range(rows):
        near = r ^ 1 if (r ^ 1) < rows else r
        for c in range(cols):
            if c in (0, cols - 1):
                to = near * cols + c
            else:
                to = r * cols + (c + 1 if c % 2 else c - 1)
            pairs.append((r * cols + c, to))
    return lax.ppermute(x, ("rows", "cols"), pairs)


def body(left, right, offsets, weight_one, bias_one, weight_two, bias_two):
    r = right.reshape(C * RH, CW)
    lr = jnp.concatenate([left.reshape(C * RH, CW), r], axis=0)
    x = packed(offsets, lr)
    even = swap(x, "cols", 0)
    odd = swap_inner(x)
    x2 = ahead(r, 2)
    x3 = ahead(r, 3)
    x4 = ahead(r, 4)
    ready = prepared(weight_one, weight_two, bias_one, bias_two)
    own = windows(offsets, even, odd, x2, x3, x4, x, lr, ready[5])
    pair = swap(own, "rows", 0)
    cross = swap(own, "rows", 1)
    out = aggregated(begun(own, ready[0], ready[5], ready[7]), pair, cross, *ready)
    return out.reshape(C, D, RH, CW)


def solution(mesh):
    return jax.shard_map(
        body,
        mesh=mesh,
        in_specs=(P(None, "rows", "cols"), P(None, "rows", "cols"), P("cols"), P(), P(), P(), P()),
        out_specs=P(None, None, "rows", "cols"),
        check_vma=False,
    )
```

```python
import jax
import jax.numpy as jnp
from jax import lax
from jax.experimental import pallas as pl
from jax.experimental.pallas import tpu as pltpu
from jax.sharding import PartitionSpec as P

C = 32
D = 48
RH = 2
CW = 128
VR = RH + 4
HR = RH + 2
VD = VR * C
HD = HR * C
OD = RH * C
KK = 768
KE = 1792
F32 = jnp.float32
BF16 = jnp.bfloat16
MIB = 1024 * 1024
VMEM = pl.BlockSpec(memory_space=pltpu.VMEM)
SMEM = pl.BlockSpec(memory_space=pltpu.SMEM)


def iota(shape, dim):
    return lax.broadcasted_iota(jnp.int32, shape, dim)


def prepare(
    w_ref, b_ref, own_ref, halo_ref, edge_ref, mid_ref, ends_ref, c1_ref, c2_ref, sel_ref
):
    zero = jnp.zeros((C, C), F32)

    def taps(base):
        return {
            (a, b, e): w_ref[base + 9 * a + 3 * b + e].astype(F32)
            for a in range(3)
            for b in range(3)
            for e in range(3)
        }

    def fill(ref, row, parts):
        for q in range(0, len(parts), 4):
            ref[row : row + C, q * C : (q + 4) * C] = jnp.concatenate(
                parts[q : q + 4], axis=1
            ).astype(BF16)

    one = taps(0)
    for r in range(HR):
        for d in range(2):
            row = (r * 2 + d) * C

            def band(rows):
                return [
                    one.get((dl - d, rl - r, e), zero)
                    for e in range(3)
                    for dl in range(4)
                    for rl in rows
                ]

            fill(own_ref, row, band((2, 3)))
            fill(halo_ref, row, band((0, 1) if r < 2 else (4, 5)))
        fill(
            edge_ref,
            r * C,
            [
                one.get((a, rl - r, e), zero)
                for e in range(3)
                for a in range(3)
                for rl in range(VR)
            ]
            + [zero] * 2,
        )
    two = taps(27)
    for d in range(4):
        for h in range(RH):
            row = (d * RH + h) * C

            def band2(deep):
                return [
                    two.get((dl - d, rl - h, e), zero)
                    for e in range(3)
                    for dl in deep
                    for rl in range(HR)
                ]

            fill(mid_ref, row, band2((2, 3)))
            fill(ends_ref, row, band2((0, 1) if d < 2 else (4, 5)))
    eye = iota((C, C), 0) == iota((C, C), 1)

    def column(b):
        b = jnp.sum(jnp.where(eye, jnp.broadcast_to(b, (C, C)), 0.0), axis=1, keepdims=True)
        return jnp.broadcast_to(b, (C, CW))

    one, two = column(b_ref[0:1, :]), column(b_ref[1:2, :])
    for p in range(8):
        c1_ref[p * C : (p + 1) * C, :] = one
        c2_ref[p * C : (p + 1) * C, :] = two
    lane = iota((128, 128), 1)
    src = iota((128, 128), 0)
    d = lane // 2
    used = d < D
    left = (lane % 2 == 1) & used
    right = (lane % 2 == 0) & used
    right_of = (
        ((3, 47 - d), (2, 47 - d)),
        ((3, 48 - d), (3, 111 - d)),
        ((1, 48 - d), (3, 112 - d)),
    )
    left_of = (((3, 50), (0, 127)), ((3, 51), (3, 114)), ((0, 0), (3, 115)))
    for e in range(3):
        for which, table in ((0, right_of), (1, left_of)):
            for t in range(4):
                hit = jnp.zeros((128, 128), jnp.bool_)
                for mask, (tile, place) in zip((left, right), table[e]):
                    if tile == t:
                        hit = hit | (mask & (src == place))
                g = 2 * e + which
                sel_ref[t * 128 : (t + 1) * 128, g * 128 : (g + 1) * 128] = jnp.where(
                    hit, 1.0, 0.0
                ).astype(BF16)


def prepared(weight_one, weight_two, bias_one, bias_two):
    return pl.pallas_call(
        prepare,
        out_shape=(
            jax.ShapeDtypeStruct((256, KK), BF16),
            jax.ShapeDtypeStruct((256, KK), BF16),
            jax.ShapeDtypeStruct((HD, KE), BF16),
            jax.ShapeDtypeStruct((256, KK), BF16),
            jax.ShapeDtypeStruct((256, KK), BF16),
            jax.ShapeDtypeStruct((256, CW), F32),
            jax.ShapeDtypeStruct((256, CW), F32),
            jax.ShapeDtypeStruct((512, 768), BF16),
        ),
        in_specs=[VMEM] * 2,
        out_specs=[VMEM] * 8,
        cost_estimate=pl.CostEstimate(flops=1000000, bytes_accessed=4000000, transcendentals=0),
        compiler_params=pltpu.CompilerParams(vmem_limit_bytes=12 * MIB),
        name="prepare",
    )(jnp.concatenate([weight_one, weight_two], axis=0), jnp.stack([bias_one, bias_two]))


def pack(off_ref, lr_ref, out_ref):
    out_ref[0:64, :] = lr_ref[64:128, :]
    k = iota((16, CW), 0)
    at = iota((16, CW), 1)
    of_left = ((k < 2) & (at == k + 126)) | ((k >= 2) & (k < 4) & (at == k - 2))
    of_right = (k >= 4) & (k < 6) & (at == k - 4)

    def columns(chosen, rows):
        return lax.dot_general(
            jnp.where(chosen, 1.0, 0.0).astype(BF16),
            rows,
            (((1,), (1,)), ((), ())),
            preferred_element_type=F32,
        )

    edge = columns(of_left, lr_ref[0:64, :]) + columns(of_right, lr_ref[64:128, :])
    o = off_ref[0]
    code = jnp.where(k == 6, o // 8, jnp.where(k == 7, o % 8, 0)).astype(F32)
    edge = jnp.concatenate([edge, jnp.zeros((16, 64), F32)], axis=1) + code
    out_ref[64:80, :] = edge.astype(BF16)


def packed(offsets, lr):
    return pl.pallas_call(
        pack,
        out_shape=jax.ShapeDtypeStruct((80, CW), BF16),
        in_specs=[SMEM, VMEM],
        out_specs=VMEM,
        compiler_params=pltpu.CompilerParams(vmem_limit_bytes=2 * MIB),
        name="pack",
    )(offsets, lr)


def cut(off_ref, even_ref, odd_ref, x2, x4, x3, xo, lr_ref, after_ref, out_ref, tiles):
    col = lax.axis_index("cols")
    final = lax.axis_size("cols") - 1
    o = off_ref[0]
    even, odd = even_ref[...], odd_ref[...]
    second = col % 2 == 1
    xl = jnp.where(second, even, odd)
    xr = jnp.where(second, odd, even)

    def scalar_of(ref):
        v = ref[64:80].astype(F32)
        return jnp.max(v[6:7, 64:128] * 8.0 + v[7:8, 64:128]).astype(jnp.int32)

    o_l = scalar_of(xl)
    o_r = scalar_of(xr)
    dst = iota((64, 64), 0)
    src = iota((64, 64), 1)
    perm = jnp.where(src == (dst % C) * RH + dst // C, 1.0, 0.0).astype(BF16)
    k = iota((16, CW), 0)
    at = iota((16, CW), 1)

    def rows(x):
        return jnp.dot(perm, x, preferred_element_type=F32)

    def placed(ref, chosen):
        edge = lax.dot_general(
            ref[64:80, 0:64],
            jnp.where(chosen, 1.0, 0.0).astype(BF16),
            (((0,), (0,)), ((), ())),
            preferred_element_type=F32,
        )
        return rows(edge.astype(BF16))

    for t, x in enumerate((x4, x3, x2, xl, xo)):
        keep = (col + (t - 4) >= 0).astype(F32)
        tiles[t] = rows(x[0:64, :]) * keep
    tiles[5] = placed(xr, (k >= 4) & (k < 6) & (at == k - 4))
    lane = iota((64, CW), 1)

    def window(start):
        t = start // CW
        s = start % CW
        back = (CW - s) % CW
        a = tiles[t]
        b = tiles[t + 1]
        return t, s, back, pltpu.roll(jnp.where(lane < s, b, a), back, 1)

    t, s, back, one = window(464 - o)
    two = pltpu.roll(jnp.where(lane < s, tiles[t + 2], tiles[t + 1]), back, 1)
    wl = window(463 - o_l)[3]
    wr = window(529 - o_r)[3]
    near = placed(xl, (k < 2) & (at == k + 50)) * (col > 0).astype(F32)
    far = placed(xr, (k >= 2) & (k < 4) & (at == k + 112)) * (col < final).astype(F32)
    border = jnp.where(lane < 50, wl, jnp.where(lane < 64, near, jnp.where(lane < 114, wr, far)))
    out_ref[0:64, :] = rows(lr_ref[0:64, :]).astype(BF16)
    out_ref[64:128, :] = one.astype(BF16)
    out_ref[128:192, :] = two.astype(BF16)
    out_ref[192:256, :] = border.astype(BF16)


def windows(offsets, even, odd, x2, x4, x3, xo, lr, after):
    return pl.pallas_call(
        cut,
        out_shape=jax.ShapeDtypeStruct((256, CW), BF16),
        in_specs=[SMEM] + [VMEM] * 7 + [pl.BlockSpec(memory_space=pl.ANY)],
        out_specs=VMEM,
        scratch_shapes=[pltpu.VMEM((6, 64, CW), F32)],
        compiler_params=pltpu.CompilerParams(vmem_limit_bytes=4 * MIB),
        name="windows",
    )(offsets, even, odd, x2, x4, x3, xo, lr, after)


def border_cells(tiles, sel):
    picked = jnp.dot(jnp.concatenate(tiles, axis=1), sel, preferred_element_type=F32)
    cells = []
    for e in range(3):
        r = picked[:, (2 * e) * CW : (2 * e + 1) * CW]
        lft = picked[:, (2 * e + 1) * CW : (2 * e + 2) * CW]
        cells.append((r * lft).astype(BF16))
    return cells


class Rows:
    def __init__(self, tiles, cells, refs):
        left, self.win0, self.win1, _ = tiles
        self.l0, self.l1, self.l2 = pltpu.roll(left, 1, 1), left, pltpu.roll(left, CW - 1, 1)
        self.z = cells[1]
        self.refs = refs
        self.lane = iota((OD, CW), 1)
        pad = jnp.zeros((OD, CW), BF16)
        for ref in refs:
            ref[0:OD, :] = pad
            ref[(D + 1) * OD : (D + 2) * OD, :] = pad
        self.held = {k: self.shifted(k) for k in (D, D + 1)}

    def shifted(self, k):
        if k == 0:
            return self.win0
        return pltpu.roll(jnp.where(self.lane < k, self.win1, self.win0), CW - k, 1)

    def disparity(self, d):
        k = D - 1 - d
        base = (d + 1) * OD
        self.held[k] = self.shifted(k)
        border = pltpu.roll(self.z, (2 * CW - 1 - 2 * d) % CW, 1)
        before, here, after = self.refs
        before[base : base + OD, :] = jnp.where(self.lane == 0, border, self.l0 * self.held[k])
        here[base : base + OD, :] = self.l1 * self.held[k + 1]
        after[base : base + OD, :] = jnp.where(
            self.lane == CW - 1, border, self.l2 * self.held.pop(k + 2)
        )


def window_rows(refs, j):
    d0 = j * 4
    return jnp.concatenate(
        [
            jnp.concatenate(
                [ref[d0 * OD : d0 * OD + 256, :], ref[(d0 + 2) * OD : (d0 + 2) * OD + 256, :]], axis=1
            )
            for ref in refs
        ],
        axis=0,
    )


def blocks(groups, conv):
    done = 0
    for j in range(D // 4):
        upto = min(D, 4 * j + 5)
        for d in range(done, upto):
            for g in groups:
                g.disparity(d)
        done = upto
        conv(j)


def begin(own, t_own, c1, sel, vol_ref, cells_ref, acc_ref):
    tiles = [own[t * 64 : t * 64 + 64, :] for t in range(4)]
    cells = border_cells(tiles, sel[...])
    for e in range(3):
        cells_ref[e] = cells[e]
    refs = [vol_ref.at[e] for e in range(3)]

    def conv(j):
        y = jnp.dot(t_own[...], window_rows(refs, j), preferred_element_type=F32)
        acc_ref[j] = y + jnp.concatenate([c1[...], c1[...]], axis=1)

    blocks([Rows(tiles, cells, refs)], conv)


def begun(own, t_own, c1, sel):
    return pl.pallas_call(
        begin,
        out_shape=(
            jax.ShapeDtypeStruct((3, (D + 2) * OD, CW), BF16),
            jax.ShapeDtypeStruct((3, OD, CW), BF16),
            jax.ShapeDtypeStruct((D // 4, 256, 256), F32),
        ),
        in_specs=[VMEM] * 4,
        out_specs=[VMEM] * 3,
        cost_estimate=pl.CostEstimate(
            flops=2 * 12 * 256 * 768 * 256, bytes_accessed=6000000, transcendentals=0
        ),
        compiler_params=pltpu.CompilerParams(vmem_limit_bytes=12 * MIB),
        name="begin",
    )(own, t_own, c1, sel)


def aggregate(
    own_vol,
    own_cells,
    acc,
    pair,
    cross,
    t_halo,
    t_edge,
    t_mid,
    t_ends,
    c1,
    c2,
    sel,
    out_ref,
    vol,
    hid,
    ready,
    sems,
):
    row = lax.axis_index("rows")
    col = lax.axis_index("cols")
    rows_last = lax.axis_size("rows") - 1
    cols_last = lax.axis_size("cols") - 1
    odd = row % 2 == 1
    no_up = row == 0
    no_down = row == rows_last
    keep_up = 1.0 - no_up.astype(F32)
    keep_down = 1.0 - no_down.astype(F32)

    def tile(t):
        part = slice(t * 64, t * 64 + 64)
        p = pair[part, :]
        x = cross[part, :]
        up = jnp.where(odd, p, x)
        down = jnp.where(odd, x, p)
        up = jnp.where(no_up, jnp.zeros_like(up), up)
        down = jnp.where(no_down, jnp.zeros_like(down), down)
        return up, down

    ups, downs = zip(*(tile(t) for t in range(4)))
    halo_cells = border_cells(
        [jnp.concatenate([u, w], axis=0) for u, w in zip(ups, downs)], sel[...]
    )
    up_cells = [z[0:OD] for z in halo_cells]
    down_cells = [z[OD:] for z in halo_cells]
    up_refs = [vol.at[0, e] for e in range(3)]
    down_refs = [vol.at[1, e] for e in range(3)]

    around = []
    for e in range(3):
        z = jnp.concatenate([up_cells[e], own_cells[e], down_cells[e]], axis=0)
        around += [pltpu.roll(z, 2, 1), z, pltpu.roll(z, CW - 2, 1)]
    around.append(jnp.zeros((KE - 9 * VD, CW), BF16))
    h = jnp.dot(t_edge[...], jnp.concatenate(around, axis=0), preferred_element_type=F32)
    h = jnp.maximum(h + c1[0:HD, :], 0.0)
    lane = iota((HD, CW), 1)
    hrow = iota((HD, CW), 0) // C
    gone = (no_up & (hrow == 0)) | (no_down & (hrow == HR - 1))
    gone = gone | ((col == 0) & (lane % 2 == 1)) | ((col == cols_last) & (lane % 2 == 0))
    hcol = jnp.where(gone, 0.0, h).astype(BF16)

    pad = jnp.zeros((HD, CW), BF16)
    for e in range(3):
        hid[e, 0:HD, :] = pad
        hid[e, (D + 1) * HD : (D + 2) * HD, :] = pad

    hl = iota((C, CW), 1)
    hfirst = hl == 0
    hlast = hl == CW - 1

    def conv_one(j):
        d0 = j * 4
        top = jnp.dot(t_halo[0:128, :], window_rows(up_refs, j), preferred_element_type=F32)
        bottom = jnp.dot(t_halo[128:256, :], window_rows(down_refs, j), preferred_element_type=F32)
        for i in range(2):
            cut = slice(i * CW, (i + 1) * CW)
            for dd in range(2):
                d = d0 + 2 * i + dd
                border = pltpu.roll(hcol, (2 * CW - 1 - 2 * d) % CW, 1)
                for r in range(HR):
                    at = (r * 2 + dd) * C
                    halo = top if r < 2 else bottom
                    ha = at % 128
                    h = acc[j, at : at + C, cut] + halo[ha : ha + C, cut]
                    h = jnp.maximum(h, 0.0)
                    if r == 0:
                        h = h * keep_up
                    if r == HR - 1:
                        h = h * keep_down
                    h = h.astype(BF16)
                    b = border[r * C : (r + 1) * C]
                    base = (d + 1) * HD + r * C
                    hid[0, base : base + C, :] = jnp.where(hfirst, b, pltpu.roll(h, 1, 1))
                    hid[1, base : base + C, :] = h
                    hid[2, base : base + C, :] = jnp.where(hlast, b, pltpu.roll(h, CW - 1, 1))

    def hidden_rows(at, *more):
        return jnp.concatenate(
            [
                jnp.concatenate([hid[e, x * HD : x * HD + 256, :] for x in (at, *more)], axis=1)
                for e in range(3)
            ],
            axis=0,
        )

    ends = {}

    def conv_two(j):
        d0 = j * 8
        mid = jnp.dot(t_mid[...], hidden_rows(d0 + 2, d0 + 6), preferred_element_type=F32)
        both = jnp.dot(t_ends[...], hidden_rows(d0, d0 + 4), preferred_element_type=F32)
        ends[2 * j] = both[:, 0:CW]
        ends[2 * j + 1] = both[:, CW:]
        return mid

    def result(j, mid):
        d0 = j * 8
        parts = []
        for i in range(2):
            low = ends.pop(2 * j + i)
            high = ends[2 * j + i + 1]
            for p in range(8):
                at = p * C
                end = low[at : at + C] if p < 4 else high[at : at + C]
                v = own_vol[1, (d0 + 4 * i + 1) * OD + at : (d0 + 4 * i + 1) * OD + at + C, :]
                a = mid[at : at + C, i * CW : (i + 1) * CW] + end + c2[0:C, :] + v.astype(F32)
                parts.append(a)
        ready[j] = jnp.swapaxes(jnp.stack(parts, axis=0).astype(BF16), 0, 1)
        copy = pltpu.make_async_copy(ready.at[j], out_ref.at[:, pl.ds(j * 16, 16), :], sems.at[j])
        copy.start()
        return copy

    blocks([Rows(ups, up_cells, up_refs), Rows(downs, down_cells, down_refs)], conv_one)
    copies = []
    mid = conv_two(0)
    for j in range(1, D // 8):
        later = conv_two(j)
        copies.append(result(j - 1, mid))
        mid = later
    ends[D // 4] = jnp.dot(t_ends[...], hidden_rows(D), preferred_element_type=F32)
    copies.append(result(D // 8 - 1, mid))
    for copy in copies:
        copy.wait()


def aggregated(first, pair, cross, t_own, *ready):
    return pl.pallas_call(
        aggregate,
        out_shape=jax.ShapeDtypeStruct((C, D * RH, CW), BF16),
        in_specs=[VMEM] * 12,
        out_specs=pl.BlockSpec(memory_space=pl.ANY),
        scratch_shapes=[
            pltpu.VMEM((2, 3, (D + 2) * OD, CW), BF16),
            pltpu.VMEM((3, (D + 2) * HD, CW), BF16),
            pltpu.VMEM((D // 8, C, 16, CW), BF16),
            pltpu.SemaphoreType.DMA((D // 8,)),
        ],
        compiler_params=pltpu.CompilerParams(vmem_limit_bytes=32 * MIB),
        name="aggregate",
    )(*first, pair, cross, *ready)


def ahead(x, by):
    n = lax.axis_size("cols")
    return lax.ppermute(x, "cols", [(i, i + by if i + by < n else n - 1 - i) for i in range(n)])


def swap(x, axis, first):
    n = lax.axis_size(axis)
    pairs = []
    for i in range(first, n + first, 2):
        a, b = i % n, (i + 1) % n
        pairs += [(a, b), (b, a)]
    return lax.ppermute(x, axis, pairs)


def swap_inner(x):
    rows, cols = lax.axis_size("rows"), lax.axis_size("cols")
    pairs = []
    for r in range(rows):
        near = r ^ 1 if (r ^ 1) < rows else r
        for c in range(cols):
            if c in (0, cols - 1):
                to = near * cols + c
            else:
                to = r * cols + (c + 1 if c % 2 else c - 1)
            pairs.append((r * cols + c, to))
    return lax.ppermute(x, ("rows", "cols"), pairs)


def body(left, right, offsets, weight_one, bias_one, weight_two, bias_two):
    lr = jnp.concatenate([left.reshape(C * RH, CW), right.reshape(C * RH, CW)], axis=0)
    x = packed(offsets, lr)
    even = swap(x, "cols", 0)
    odd = swap_inner(x)
    x2 = ahead(x, 2)
    x3 = ahead(x, 3)
    x4 = ahead(x, 4)
    ready = prepared(weight_one, weight_two, bias_one, bias_two)
    own = windows(offsets, even, odd, x2, x4, x3, x, lr, ready[5])
    pair = swap(own, "rows", 0)
    cross = swap(own, "rows", 1)
    out = aggregated(begun(own, ready[0], ready[5], ready[7]), pair, cross, *ready)
    return out.reshape(C, D, RH, CW)


def solution(mesh):
    return jax.shard_map(
        body,
        mesh=mesh,
        in_specs=(P(None, "rows", "cols"), P(None, "rows", "cols"), P("cols"), P(), P(), P(), P()),
        out_specs=P(None, None, "rows", "cols"),
        check_vma=False,
    )
```
